32 devices in a mesh: nodes: 8 (over z, y), heads: 4 (over x, core).
Axes of the slice: x: 2, y: 2, z: 4, core: 2. Of those that a mesh axis runs over, the one named last changes fastest.
Arguments:
- node_feats: bfloat16 [2048, 512], P('nodes'), may hold values from -6 to 6
- node_types: int32 [2048], P('nodes'), may hold values from 0 to 4
- queries: bfloat16 [2048, 512], P('nodes', 'heads'), may hold values from -6 to 6
- key_rows: bfloat16 [2048, 512], P('nodes', 'heads'), may hold values from -6 to 6
- value_rows: bfloat16 [2048, 512], P('nodes', 'heads'), may hold values from -6 to 6
- halo_keys: bfloat16 [512, 512], P('nodes', 'heads'), may hold values from -6 to 6
- halo_values: bfloat16 [512, 512], P('nodes', 'heads'), may hold values from -6 to 6
- halo_rows: int32 [512], P('nodes'), may hold values from 0 to 256, as said below
- edge_tiles: int32 [320, 3], P('nodes'), may hold values from 0 to 14, as said below
- grad_output: bfloat16 [2048, 512], P('nodes', 'heads'), may hold values from -6 to 6
- proj_weight: bfloat16 [3, 5, 512, 512], P(None, None, None, 'heads'), may hold values from -0.25 to 0.25
- rel_weight: bfloat16 [2, 15, 8, 64, 64], P(None, None, 'heads'), may hold values from -0.75 to 0.75
- rel_prior: float32 [15, 8], P(None, 'heads'), may hold values from 0.5 to 2
Outputs:
- grad_feats: bfloat16 [2048, 512], P('nodes', 'heads')
- grad_proj: float32 [512, 3, 5, 512], P('nodes', None, None, 'heads')
- grad_rel: float32 [2, 15, 8, 64, 64], P(None, None, 'heads')
- grad_prior: float32 [15, 8], P(None, 'heads')
The draws below stay inside these ranges and needn't reach their ends.
Inputs may be any that keep to these rules, and one draw needn't show every extreme that they name: `halo_rows`: slab s's halo is 8 blocks of 8 slots, block j holding distinct rows of slab j first and 256 in its empty slots; block s of slab s is empty; one slab t is copied in full: every slab other than t holds 8 distinct rows of t in block t; every other block of another slab holds between 1 and 8 rows. `edge_tiles`: an entry is live when its destination tile is below 4, and is empty with destination 256 // 64, source 0 and relation 0. A source tile below 4 lies among the slab's own rows, the others among its halo slots. Every destination tile has a live entry whose source lies among the own rows. Some slab has every entry live.
All inputs are finite; a program needn't handle non-finite values.
Results may differ from the reference program's by a relative error of at most 0.012.
The reference program's roundings to bfloat16 on the way count: a program that leaves them out, or rounds other values in their place, can miss the bound.
Values may be sent and summed in bfloat16 or wider, within the bound.
A program may use at most 64 MiB of HBM per device.

```python
import math
import jax
import jax.numpy as jnp
from jax import lax

D = 512
HEADS = 8
HEAD_DIM = 64
TYPES = 5
RELS = 15
TILE = 64
ROWS = 256
CAP = 8
HALO = 64
TILES_DEV = 40
NODES = 2048
N_NODES = 8


def draw_halo_rows(key, part):
    key = jax.random.fold_in(key, 11)
    first, second, third = jax.random.split(key, 3)
    counts = jax.random.randint(first, (N_NODES, N_NODES), 1, CAP + 1)
    target = jax.random.randint(second, (), 0, N_NODES)
    sender = jnp.arange(N_NODES)[:, None]
    owners = jnp.arange(N_NODES)[None, :]
    counts = jnp.where(owners == target, CAP, counts)
    counts = jnp.where(sender == owners, 0, counts)
    scores = jax.random.randint(third, (N_NODES, N_NODES, ROWS), 0, 65536) * ROWS + jnp.arange(ROWS)
    ranked = jnp.argsort(scores, axis=-1)[..., :CAP]
    slot_index = jnp.arange(CAP)
    row_ids = jnp.where(slot_index[None, None, :] < counts[..., None], ranked, ROWS)
    return row_ids.reshape(-1).astype(jnp.int32)


def draw_edge_tiles(key, part):
    key = jax.random.fold_in(key, 23)
    keys_list = jax.random.split(key, 7)
    dest_tiles = ROWS // TILE
    source_tiles = dest_tiles + HALO // TILE
    spread = 1024
    picks = jax.random.randint(keys_list[0], (N_NODES,), 0, spread)
    live_count = dest_tiles + picks * (picks + spread) * (TILES_DEV - dest_tiles) // (2 * spread * spread)
    busiest = jax.random.randint(keys_list[1], (), 0, N_NODES)
    live_count = jnp.where(jnp.arange(N_NODES) == busiest, TILES_DEV, live_count)
    entry = jnp.arange(TILES_DEV)[None, :]
    target = jnp.where(entry < dest_tiles, entry, jax.random.randint(keys_list[2], (N_NODES, TILES_DEV), 0, dest_tiles))
    source = jnp.where(entry < dest_tiles, jax.random.randint(keys_list[3], (N_NODES, TILES_DEV), 0, dest_tiles), jax.random.randint(keys_list[4], (N_NODES, TILES_DEV), 0, source_tiles))
    relation = jax.random.randint(keys_list[5], (N_NODES, TILES_DEV), 0, RELS)
    live_mask = entry < live_count[:, None]
    target = jnp.where(live_mask, target, dest_tiles)
    source = jnp.where(live_mask, source, 0)
    relation = jnp.where(live_mask, relation, 0)
    orders = jax.vmap(lambda sub: jax.random.permutation(sub, TILES_DEV))(jax.random.split(keys_list[6], N_NODES))
    stacked = jnp.stack([target, source, relation], axis=-1)
    shuffled = jnp.take_along_axis(stacked, orders[:, :, None], axis=1)
    return shuffled.reshape(N_NODES * TILES_DEV, 3).astype(jnp.int32)


def place_ends(array, own_key, smallest, high):
    index_at = [jax.random.randint(jax.random.fold_in(own_key, axis), (), 0, length) for axis, length in enumerate(array.shape)]
    longest = array.shape.index(max(array.shape))
    next_to = index_at[:longest] + [(index_at[longest] + 1) % array.shape[longest]] + index_at[longest + 1:]
    return array.at[tuple(index_at)].set(smallest).at[tuple(next_to)].set(high)


def spiked(array, own_key, source, target, blocks, factor):
    owner, partner = [(jnp.arange(array.shape[position]) // (array.shape[position] // blocks)).reshape([-1 if axis == position else 1 for axis in range(array.ndim)]) for position in (source, target)]
    chosen = jax.random.permutation(own_key, blocks)[partner]
    strong = (owner == chosen) | (owner == (partner + blocks // 2) % blocks)
    return jnp.where(strong, factor * array, array)


def steps_of(own_key, shape, shards, least, largest):
    def one(position, blocks):
        draws = jax.random.uniform(jax.random.fold_in(jax.random.fold_in(own_key, 6), position), (blocks,), jnp.float32, least / len(shards), largest / len(shards))
        return jnp.repeat(jnp.exp(draws), shape[position] // blocks).reshape((-1,) + (1,) * (len(shape) - position - 1))

    loudness = one(*shards[0])
    for cut in shards[1:]:
        loudness = loudness * one(*cut)
    return loudness


def normal_values(rng, dims, scale, reach, shards=(), held_as=jnp.bfloat16):
    drawn = jax.random.normal(rng, dims, jnp.float32) * scale
    if len(shards) > 0:
        drawn = steps_of(rng, dims, shards, -0.22, 0.18) * drawn
    return jnp.clip(drawn, min=-reach, max=reach).astype(held_as)


def heavy_noise(stream_key, dims, width, most, cuts, heavy, held_as=jnp.bfloat16):
    values = width * jax.random.normal(stream_key, dims, jnp.float32)
    if cuts:
        values = values * steps_of(stream_key, dims, cuts, -0.22, 0.18)
    return jnp.clip(spiked(values, jax.random.fold_in(stream_key, 3), *heavy), -most, most).astype(held_as)


def setup_inputs(seed: int = 0) -> dict:
    splits = jax.random.split(jax.random.key(seed), 14)
    return {
        "node_feats": heavy_noise(splits[0], (NODES, D), 1.0, 6.0, ((0, 8),), (0, 1, 8, 2.0)),
        "node_types": place_ends(jax.random.randint(splits[1], (NODES,), 0, TYPES), jax.random.fold_in(splits[1], 1), 0, TYPES - 1).astype(jnp.int32),
        "queries": normal_values(splits[2], (NODES, D), 1.0, 6.0, ((0, 8), (1, 4))),
        "key_rows": normal_values(splits[3], (NODES, D), 1.0, 6.0, ((0, 8), (1, 4))),
        "value_rows": normal_values(splits[4], (NODES, D), 1.0, 6.0, ((0, 8), (1, 4))),
        "halo_keys": normal_values(splits[5], (N_NODES * HALO, D), 1.0, 6.0, ((0, 8), (1, 4))),
        "halo_values": normal_values(splits[6], (N_NODES * HALO, D), 1.0, 6.0, ((0, 8), (1, 4))),
        "halo_rows": draw_halo_rows(jax.random.fold_in(splits[13], 71), 0),
        "edge_tiles": draw_edge_tiles(jax.random.fold_in(splits[13], 71), 0),
        "grad_output": normal_values(splits[9], (NODES, D), 1.0, 6.0, ((0, 8), (1, 4))),
        "proj_weight": normal_values(splits[10], (3, TYPES, D, D), D ** -0.5, 0.25, ((3, 4),)),
        "rel_weight": normal_values(splits[11], (2, RELS, HEADS, HEAD_DIM, HEAD_DIM), HEAD_DIM ** -0.5, 0.75, ((2, 4),)),
        "rel_prior": jnp.clip(jnp.exp(math.log(2.0) - 1.3862944 * jax.random.uniform(splits[12], (RELS, HEADS), jnp.float32) ** steps_of(splits[12], (RELS, HEADS), ((1, 4),), -0.2, 0.2)), 0.5, 2.0),
    }


def attend(queries, key_rows, value_rows, valid, grad_output, edge_tiles, rel_weight, rel_prior):
    head_count = queries.shape[1]
    head_dim = queries.shape[2]
    dest_tiles = queries.shape[0] // TILE
    source_tiles = key_rows.shape[0] // TILE
    inv_root = head_dim ** -0.5
    query_tiles = queries.reshape(dest_tiles, TILE, head_count, head_dim).astype(jnp.float32)
    key_tiles = key_rows.reshape(source_tiles, TILE, head_count, head_dim).astype(jnp.float32)
    value_tiles = value_rows.reshape(source_tiles, TILE, head_count, head_dim).astype(jnp.float32)
    grad_tiles = grad_output.reshape(dest_tiles, TILE, head_count, head_dim).astype(jnp.float32)
    target = edge_tiles[:, 0]
    source = edge_tiles[:, 1]
    relation = edge_tiles[:, 2]
    live_mask = (target < dest_tiles).astype(jnp.float32)
    clipped = jnp.minimum(target, dest_tiles - 1)
    query_edge = query_tiles[clipped]
    key_edge = key_tiles[source]
    value_edge = value_tiles[source]
    grad_edge = grad_tiles[clipped]
    columns = valid.reshape(source_tiles, TILE)[source] * live_mask[:, None]
    score_weight = rel_weight[0][relation].astype(jnp.float32)
    message_weight = rel_weight[1][relation].astype(jnp.float32)
    prior_edge = rel_prior[relation]
    key_mixed = jnp.einsum('etha,ehab->ethb', key_edge, score_weight).astype(jnp.bfloat16).astype(jnp.float32)
    message = jnp.einsum('etha,ehab->ethb', value_edge, message_weight).astype(jnp.bfloat16).astype(jnp.float32)
    logits = jnp.einsum('etha,esha->ehts', query_edge, key_mixed) * inv_root
    exp_scores = jnp.exp(logits * prior_edge[:, :, None, None]) * columns[:, None, None, :]
    owner_map = (target[:, None] == jnp.arange(dest_tiles)[None, :]).astype(jnp.float32)
    denominator = jnp.einsum('ed,eht->dht', owner_map, jnp.sum(exp_scores, axis=-1), precision=lax.Precision.HIGHEST)
    softmax = exp_scores / denominator[clipped][..., None]
    prob_bf = softmax.astype(jnp.bfloat16).astype(jnp.float32)
    partial_value = jnp.einsum('ehts,eshb->ethb', prob_bf, message)
    output = jnp.einsum('ed,ethb->dthb', owner_map, partial_value, precision=lax.Precision.HIGHEST)
    deltas = jnp.sum(grad_tiles * output, axis=-1)
    delta_edge = jnp.transpose(deltas[clipped], (0, 2, 1))
    prob_grad = jnp.einsum('ethb,eshb->ehts', grad_edge, message)
    score_grad = softmax * (prob_grad - delta_edge[..., None])
    logit_grad = (score_grad * (prior_edge * inv_root)[:, :, None, None]).astype(jnp.bfloat16).astype(jnp.float32)
    query_edge_grad = jnp.einsum('ehts,esha->etha', logit_grad, key_mixed)
    key_mixed_grad = jnp.einsum('ehts,etha->esha', logit_grad, query_edge).astype(jnp.bfloat16).astype(jnp.float32)
    message_grad = jnp.einsum('ehts,ethb->eshb', prob_bf, grad_edge).astype(jnp.bfloat16).astype(jnp.float32)
    key_edge_grad = jnp.einsum('eshb,ehab->esha', key_mixed_grad, score_weight)
    value_edge_grad = jnp.einsum('eshb,ehab->esha', message_grad, message_weight)
    score_weight_grad = jnp.einsum('esha,eshb->ehab', key_edge, key_mixed_grad)
    message_weight_grad = jnp.einsum('esha,eshb->ehab', value_edge, message_grad)
    prior_edge_grad = jnp.sum(score_grad * logits, axis=(2, 3))
    source_map = (source[:, None] == jnp.arange(source_tiles)[None, :]).astype(jnp.float32) * live_mask[:, None]
    query_grad = jnp.einsum('ed,etha->dtha', owner_map, query_edge_grad, precision=lax.Precision.HIGHEST)
    key_grad = jnp.einsum('ej,esha->jsha', source_map, key_edge_grad, precision=lax.Precision.HIGHEST)
    value_grad = jnp.einsum('ej,esha->jsha', source_map, value_edge_grad, precision=lax.Precision.HIGHEST)
    chooser = (relation[:, None] == jnp.arange(RELS)[None, :]).astype(jnp.float32)
    relation_grad = jnp.stack([
        jnp.einsum('er,ehab->rhab', chooser, score_weight_grad, precision=lax.Precision.HIGHEST),
        jnp.einsum('er,ehab->rhab', chooser, message_weight_grad, precision=lax.Precision.HIGHEST)])
    prior_grad = jnp.einsum('er,eh->rh', chooser, prior_edge_grad, precision=lax.Precision.HIGHEST)
    return (query_grad.reshape(dest_tiles * TILE, head_count, head_dim),
            key_grad.reshape(source_tiles * TILE, head_count, head_dim),
            value_grad.reshape(source_tiles * TILE, head_count, head_dim),
            relation_grad, prior_grad)


def reference(node_feats, node_types, queries, key_rows, value_rows, halo_keys, halo_values, halo_rows, edge_tiles, grad_output, proj_weight, rel_weight, rel_prior):
    head_dim = D // HEADS
    slab_count = N_NODES

    def by_heads(matrix, count):
        return matrix.reshape(slab_count, count, HEADS, head_dim)

    def per_slab(items):
        query_slab, key_slab, value_slab, halo_key_slab, halo_value_slab, halo_slab, tile_slab, grad_slab = items
        valid = jnp.concatenate([jnp.ones((ROWS,), jnp.float32), (halo_slab < ROWS).astype(jnp.float32)])
        return attend(query_slab, jnp.concatenate([key_slab, halo_key_slab]),
                      jnp.concatenate([value_slab, halo_value_slab]), valid, grad_slab,
                      tile_slab, rel_weight, rel_prior)

    query_grad, key_grad, value_grad, relation_grad, prior_grad = lax.map(per_slab, (
        by_heads(queries, ROWS), by_heads(key_rows, ROWS), by_heads(value_rows, ROWS),
        by_heads(halo_keys, HALO), by_heads(halo_values, HALO),
        halo_rows.reshape(slab_count, HALO), edge_tiles.reshape(slab_count, TILES_DEV, 3),
        by_heads(grad_output, ROWS)))
    query_bf = query_grad.reshape(NODES, D).astype(jnp.bfloat16)
    key_own = key_grad[:, :ROWS].reshape(NODES, D).astype(jnp.bfloat16)
    value_own = value_grad[:, :ROWS].reshape(NODES, D).astype(jnp.bfloat16)
    key_halo = key_grad[:, ROWS:].reshape(slab_count * HALO, D).astype(jnp.bfloat16)
    value_halo = value_grad[:, ROWS:].reshape(slab_count * HALO, D).astype(jnp.bfloat16)
    slot_index = jnp.arange(slab_count * HALO).astype(jnp.int32)
    owners = (slot_index % HALO) // CAP
    places = jnp.where(halo_rows < ROWS, owners * ROWS + halo_rows, NODES).astype(jnp.int32)
    key_back = jnp.zeros((NODES, D), jnp.float32).at[places].add(key_halo.astype(jnp.float32), mode="drop")
    value_back = jnp.zeros((NODES, D), jnp.float32).at[places].add(value_halo.astype(jnp.float32), mode="drop")
    gradients = (query_bf.astype(jnp.float32), key_own.astype(jnp.float32) + key_back,
                 value_own.astype(jnp.float32) + value_back)
    feats_wide = node_feats.astype(jnp.float32)
    grad_feats = jnp.zeros((NODES, D), jnp.float32)
    blocks = []
    for proj_index in range(3):
        row_blocks = []
        for type_index in range(TYPES):
            masked = gradients[proj_index] * (node_types == type_index).astype(jnp.float32)[:, None]
            weight_wide = proj_weight[proj_index, type_index].astype(jnp.float32)
            grad_feats = grad_feats + jnp.dot(masked, weight_wide.T, precision=lax.Precision.HIGHEST)
            row_blocks.append(jnp.dot(feats_wide.T, masked, precision=lax.Precision.HIGHEST))
        blocks.append(jnp.stack(row_blocks))
    grad_proj = jnp.transpose(jnp.stack(blocks), (2, 0, 1, 3))
    return grad_feats.astype(jnp.bfloat16), grad_proj, jnp.sum(relation_grad, axis=0), jnp.sum(prior_grad, axis=0)
```

```python
import functools

import jax
import jax.numpy as jnp
from jax import lax
from jax.experimental import pallas as pl
from jax.experimental.pallas import tpu as pltpu
from jax.sharding import PartitionSpec as P

TYPES = 5
RELS = 15
TILE = 64
CAP = 8
BF = jnp.bfloat16
F32 = jnp.float32
VMEM = pl.BlockSpec(memory_space=pltpu.VMEM)
SMEM = pl.BlockSpec(memory_space=pltpu.SMEM)


def mm(left, right, left_dim, right_dim):
    return lax.dot_general(
        left, right, (((left_dim,), (right_dim,)), ((), ())), preferred_element_type=F32
    )


def attend_kernel(
    dest_tiles,
    source_tiles,
    edge_count,
    unroll,
    edge_ref,
    prior_ref,
    query_ref,
    key_ref,
    value_ref,
    halo_key_ref,
    halo_value_ref,
    grad_ref,
    valid_ref,
    weight_ref,
    query_out,
    key_out,
    value_out,
    rel_out,
    prior_out,
    keys,
    values,
    wide,
    mixed,
    message,
    logits,
    scores,
    prob_grad,
    sums,
    deltas,
    query_acc,
    key_acc,
    value_acc,
):
    own = dest_tiles * TILE
    width = 2 * TILE
    keys[:own] = key_ref[...]
    keys[own:] = halo_key_ref[...]
    values[:own] = value_ref[...]
    values[own:] = halo_value_ref[...]
    blank = jnp.zeros((TILE, TILE), BF)
    for side in range(2):
        for rel in range(RELS):
            wide[side, rel] = jnp.concatenate(
                [
                    jnp.concatenate([weight_ref[side, rel, 0], blank], axis=1),
                    jnp.concatenate([blank, weight_ref[side, rel, 1]], axis=1),
                ],
                axis=0,
            )
    for ref in (sums, deltas, query_acc, key_acc, value_acc, rel_out, prior_out):
        ref[...] = jnp.zeros_like(ref)
    first = lax.broadcasted_iota(jnp.int32, (TILE, width), 1) < TILE
    first_row = lax.broadcasted_iota(jnp.int32, (1, width), 1) < TILE
    low = first.astype(F32).astype(BF)
    high = (1.0 - first.astype(F32)).astype(BF)

    def stacked(both):
        return jnp.concatenate([both * low, both * high], axis=0)

    def diagonal(square):
        return jnp.where(first, square[:TILE], square[TILE:])

    def head_sum(total):
        left = jnp.sum(jnp.where(first, total, 0.0), axis=1, keepdims=True)
        right = jnp.sum(jnp.where(first, 0.0, total), axis=1, keepdims=True)
        return jnp.where(first, left, right)

    def entry(index):
        target = edge_ref[3 * index]
        live = target < dest_tiles
        dest = jnp.minimum(target, dest_tiles - 1)
        source = edge_ref[3 * index + 1]
        rel = edge_ref[3 * index + 2]
        prior = jnp.where(first_row, prior_ref[2 * rel], prior_ref[2 * rel + 1])
        return live, dest, source, rel, prior

    def rows_of(tile):
        return pl.ds(pl.multiple_of(tile * TILE, TILE), TILE)

    def score_step(step, carry):
        found = []
        for part in range(unroll):
            index = step * unroll + part
            live, dest, source, rel, prior = entry(index)
            at = rows_of(dest)
            mixed_now = mm(keys[rows_of(source)], wide[0, rel], 1, 0).astype(BF)
            message_now = mm(values[rows_of(source)], wide[1, rel], 1, 0).astype(BF)
            logit = mm(query_ref[at], stacked(mixed_now), 1, 1) * (TILE**-0.5)
            grad = mm(grad_ref[at], stacked(message_now), 1, 1)
            keep = valid_ref[source][:1] * jnp.where(live, 1.0, 0.0)
            score = jnp.where(keep > 0.0, jnp.exp(logit * prior), 0.0)
            found.append((index, dest, mixed_now, message_now, logit, grad, score))
        for index, dest, mixed_now, message_now, logit, grad, score in found:
            mixed[index] = mixed_now
            message[index] = message_now
            logits[index] = logit
            prob_grad[index] = grad
            scores[index] = score
            sums[dest] += score
        return carry

    lax.fori_loop(0, edge_count // unroll, score_step, 0)
    for tile in range(dest_tiles):
        sums[tile] = 1.0 / head_sum(sums[tile])

    def delta_step(step, carry):
        found = []
        for part in range(unroll):
            index = step * unroll + part
            _, dest, _, _, _ = entry(index)
            soft = scores[index] * sums[dest]
            found.append((index, dest, soft, soft.astype(BF).astype(F32) * prob_grad[index]))
        for index, dest, soft, product in found:
            scores[index] = soft
            deltas[dest] += product
        return carry

    lax.fori_loop(0, edge_count // unroll, delta_step, 0)
    for tile in range(dest_tiles):
        deltas[tile] = head_sum(deltas[tile])

    def grad_step(step, carry):
        found = []
        for part in range(unroll):
            index = step * unroll + part
            _, dest, source, rel, prior = entry(index)
            at = rows_of(dest)
            soft = scores[index]
            score_grad = soft * (prob_grad[index] - deltas[dest])
            prior_now = jnp.sum(score_grad * logits[index], axis=0, keepdims=True)
            logit_grad = (score_grad * (prior * (TILE**-0.5))).astype(BF)
            query_now = mm(logit_grad, stacked(mixed[index]), 1, 0)
            mixed_grad = diagonal(mm(logit_grad, query_ref[at], 0, 0)).astype(BF)
            message_grad = diagonal(mm(soft.astype(BF), grad_ref[at], 0, 0)).astype(BF)
            key_now = mm(mixed_grad, wide[0, rel], 1, 1)
            value_now = mm(message_grad, wide[1, rel], 1, 1)
            score_weight = diagonal(mm(keys[rows_of(source)], mixed_grad, 0, 0))
            message_weight = diagonal(mm(values[rows_of(source)], message_grad, 0, 0))
            found.append(
                (
                    dest,
                    source,
                    rel,
                    prior_now,
                    query_now,
                    key_now,
                    value_now,
                    score_weight,
                    message_weight,
                )
            )
        for dest, source, rel, prior_now, query_now, key_now, value_now, one, two in found:
            prior_out[rel] += prior_now
            query_acc[dest] += query_now
            key_acc[source] += key_now
            value_acc[source] += value_now
            rel_out[0, rel] += one
            rel_out[1, rel] += two
        return carry

    lax.fori_loop(0, edge_count // unroll, grad_step, 0)
    for tile in range(dest_tiles):
        query_out[tile * TILE : (tile + 1) * TILE] = query_acc[tile].astype(BF)
    for tile in range(source_tiles):
        key_out[tile * TILE : (tile + 1) * TILE] = key_acc[tile].astype(BF)
        value_out[tile * TILE : (tile + 1) * TILE] = value_acc[tile].astype(BF)


def attend(
    queries,
    key_rows,
    value_rows,
    halo_keys,
    halo_values,
    halo_rows,
    grad_output,
    edge_tiles,
    rel_weight,
    rel_prior,
):
    own, width = queries.shape
    halo = halo_keys.shape[0]
    edges = edge_tiles.shape[0]
    dest_tiles = own // TILE
    source_tiles = (own + halo) // TILE
    unroll = 4 if edges % 4 == 0 else 1
    valid = jnp.concatenate([jnp.ones((own,), F32), (halo_rows < own).astype(F32)])
    valid = valid.reshape(source_tiles, 1, TILE)
    valid = jnp.broadcast_to(jnp.concatenate([valid, valid], axis=2), (source_tiles, 8, width))
    per_edge = (edges, TILE, width)
    per_dest = (dest_tiles, TILE, width)
    per_source = (source_tiles, TILE, width)
    return pl.pallas_call(
        functools.partial(attend_kernel, dest_tiles, source_tiles, edges, unroll),
        out_shape=(
            jax.ShapeDtypeStruct((own, width), BF),
            jax.ShapeDtypeStruct((own + halo, width), BF),
            jax.ShapeDtypeStruct((own + halo, width), BF),
            jax.ShapeDtypeStruct((2, RELS, TILE, width), F32),
            jax.ShapeDtypeStruct((RELS, 1, width), F32),
        ),
        in_specs=[SMEM] * 2 + [VMEM] * 8,
        out_specs=(VMEM,) * 5,
        scratch_shapes=[
            pltpu.VMEM((own + halo, width), BF),
            pltpu.VMEM((own + halo, width), BF),
            pltpu.VMEM((2, RELS, width, width), BF),
            pltpu.VMEM(per_edge, BF),
            pltpu.VMEM(per_edge, BF),
            pltpu.VMEM(per_edge, F32),
            pltpu.VMEM(per_edge, F32),
            pltpu.VMEM(per_edge, F32),
            pltpu.VMEM(per_dest, F32),
            pltpu.VMEM(per_dest, F32),
            pltpu.VMEM(per_dest, F32),
            pltpu.VMEM(per_source, F32),
            pltpu.VMEM(per_source, F32),
        ],
        compiler_params=pltpu.CompilerParams(vmem_limit_bytes=48 * 1024 * 1024),
        name="attend",
    )(
        edge_tiles.reshape(-1),
        rel_prior.reshape(-1),
        queries,
        key_rows,
        value_rows,
        halo_keys,
        halo_values,
        grad_output,
        valid,
        rel_weight,
    )


def per_device(
    node_feats,
    node_types,
    queries,
    key_rows,
    value_rows,
    halo_keys,
    halo_values,
    halo_rows,
    edge_tiles,
    grad_output,
    proj_weight,
    rel_weight,
    rel_prior,
):
    own_count = node_feats.shape[0]
    halo_count = halo_keys.shape[0]
    local_width = queries.shape[1]
    query_grad, key_grad, value_grad, relation_grad, prior_grad = attend(
        queries,
        key_rows,
        value_rows,
        halo_keys,
        halo_values,
        halo_rows,
        grad_output,
        edge_tiles,
        rel_weight,
        rel_prior,
    )
    relation_grad = jnp.transpose(
        relation_grad.reshape(2, RELS, TILE, 2, TILE), (0, 1, 3, 2, 4)
    )
    prior_grad = jnp.sum(prior_grad.reshape(RELS, 2, TILE), axis=-1)
    outgoing = jnp.concatenate([key_grad[own_count:], value_grad[own_count:]], axis=1)
    incoming, incoming_rows = (
        lax.all_to_all(outgoing, "nodes", split_axis=0, concat_axis=0, tiled=True),
        lax.all_to_all(halo_rows, "nodes", split_axis=0, concat_axis=0, tiled=True),
    )
    type_range = jnp.arange(TYPES)
    own_types = (node_types[:, None] == type_range[None, :]).astype(BF)
    own_stack = jnp.stack([query_grad, key_grad[:own_count], value_grad[:own_count]], axis=1)
    own_blocks = own_types[:, None, :, None] * own_stack[:, :, None, :]
    clamped = jnp.minimum(incoming_rows, own_count - 1)
    halo_types = (node_types[clamped][:, None] == type_range[None, :]).astype(BF)
    halo_types = halo_types * (incoming_rows < own_count).astype(BF)[:, None]
    halo_blocks = (
        halo_types[:, None, :, None] * incoming.reshape(halo_count, 2, local_width)[:, :, None, :]
    )
    contract = (((1, 2, 3), (0, 1, 3)), ((), ()))
    feat_grad = lax.dot_general(own_blocks, proj_weight, contract, preferred_element_type=F32)
    halo_feat = lax.dot_general(halo_blocks, proj_weight[1:], contract, preferred_element_type=F32)
    feat_grad = feat_grad.at[incoming_rows].add(halo_feat, mode="drop")
    grad_feats = lax.psum_scatter(feat_grad, "heads", scatter_dimension=1, tiled=True).astype(BF)
    own_part = jnp.einsum("ri,rptk->iptk", node_feats, own_blocks, preferred_element_type=F32)
    halo_part = jnp.einsum(
        "ri,rptk->iptk", node_feats[clamped], halo_blocks, preferred_element_type=F32
    )
    grad_proj = lax.psum_scatter(
        own_part.at[:, 1:].add(halo_part), "nodes", scatter_dimension=0, tiled=True
    )
    grad_rel, grad_prior = lax.psum((relation_grad, prior_grad), "nodes")
    return (grad_feats, grad_proj, grad_rel, grad_prior)


def solution(mesh):
    return jax.shard_map(
        per_device,
        mesh=mesh,
        in_specs=(
            P("nodes", None),
            P("nodes"),
            P("nodes", "heads"),
            P("nodes", "heads"),
            P("nodes", "heads"),
            P("nodes", "heads"),
            P("nodes", "heads"),
            P("nodes"),
            P("nodes", None),
            P("nodes", "heads"),
            P(None, None, None, "heads"),
            P(None, None, "heads", None, None),
            P(None, "heads"),
        ),
        out_specs=(
            P("nodes", "heads"),
            P("nodes", None, None, "heads"),
            P(None, None, "heads", None, None),
            P(None, "heads"),
        ),
        check_vma=False,
    )
```

```python
import functools

import jax
import jax.numpy as jnp
from jax import lax
from jax.experimental import pallas as pl
from jax.experimental.pallas import tpu as pltpu
from jax.sharding import PartitionSpec as P

TYPES = 5
RELS = 15
TILE = 64
CAP = 8
BF = jnp.bfloat16
F32 = jnp.float32
VMEM = pl.BlockSpec(memory_space=pltpu.VMEM)
SMEM = pl.BlockSpec(memory_space=pltpu.SMEM)


def mm(left, right, left_dim, right_dim):
    return lax.dot_general(
        left, right, (((left_dim,), (right_dim,)), ((), ())), preferred_element_type=F32
    )


def attend_kernel(
    dest_tiles,
    source_tiles,
    edge_count,
    unroll,
    edge_ref,
    prior_ref,
    query_ref,
    key_ref,
    value_ref,
    halo_key_ref,
    halo_value_ref,
    grad_ref,
    valid_ref,
    slot_ref,
    weight_ref,
    pack_out,
    halo_out,
    rel_out,
    prior_out,
    keys,
    values,
    wide,
    mixed,
    message,
    logits,
    scores,
    prob_grad,
    sums,
    deltas,
    query_acc,
    key_acc,
    value_acc,
):
    own = dest_tiles * TILE
    width = 2 * TILE
    keys[:own] = key_ref[...]
    keys[own:] = halo_key_ref[...]
    values[:own] = value_ref[...]
    values[own:] = halo_value_ref[...]
    blank = jnp.zeros((TILE, TILE), BF)
    for side in range(2):
        for rel in range(RELS):
            wide[side, rel] = jnp.concatenate(
                [
                    jnp.concatenate([weight_ref[side, rel, 0], blank], axis=1),
                    jnp.concatenate([blank, weight_ref[side, rel, 1]], axis=1),
                ],
                axis=0,
            )
    for ref in (sums, deltas, query_acc, key_acc, value_acc, rel_out, prior_out):
        ref[...] = jnp.zeros_like(ref)
    first = lax.broadcasted_iota(jnp.int32, (TILE, width), 1) < TILE
    first_row = lax.broadcasted_iota(jnp.int32, (1, width), 1) < TILE
    low = first.astype(F32).astype(BF)
    high = (1.0 - first.astype(F32)).astype(BF)

    def stacked(both):
        return jnp.concatenate([both * low, both * high], axis=0)

    def diagonal(square):
        return jnp.where(first, square[:TILE], square[TILE:])

    def head_sum(total):
        left = jnp.sum(jnp.where(first, total, 0.0), axis=1, keepdims=True)
        right = jnp.sum(jnp.where(first, 0.0, total), axis=1, keepdims=True)
        return jnp.where(first, left, right)

    def entry(index):
        target = edge_ref[3 * index]
        live = target < dest_tiles
        dest = jnp.minimum(target, dest_tiles - 1)
        source = edge_ref[3 * index + 1]
        rel = edge_ref[3 * index + 2]
        prior = jnp.where(first_row, prior_ref[2 * rel], prior_ref[2 * rel + 1])
        return live, dest, source, rel, prior

    def rows_of(tile):
        return pl.ds(pl.multiple_of(tile * TILE, TILE), TILE)

    def score_step(step, carry):
        found = []
        for part in range(unroll):
            index = step * unroll + part
            live, dest, source, rel, prior = entry(index)
            at = rows_of(dest)
            mixed_now = mm(keys[rows_of(source)], wide[0, rel], 1, 0).astype(BF)
            message_now = mm(values[rows_of(source)], wide[1, rel], 1, 0).astype(BF)
            logit = mm(query_ref[at], stacked(mixed_now), 1, 1) * (TILE**-0.5)
            grad = mm(grad_ref[at], stacked(message_now), 1, 1)
            keep = valid_ref[source][:1] * jnp.where(live, 1.0, 0.0)
            score = jnp.where(keep > 0.0, jnp.exp(logit * prior), 0.0)
            found.append((index, dest, mixed_now, message_now, logit, grad, score))
        for index, dest, mixed_now, message_now, logit, grad, score in found:
            mixed[index] = mixed_now
            message[index] = message_now
            logits[index] = logit
            prob_grad[index] = grad
            scores[index] = score
            sums[dest] += score
        return carry

    lax.fori_loop(0, edge_count // unroll, score_step, 0)
    for tile in range(dest_tiles):
        sums[tile] = 1.0 / head_sum(sums[tile])

    def delta_step(step, carry):
        found = []
        for part in range(unroll):
            index = step * unroll + part
            _, dest, _, _, _ = entry(index)
            soft = scores[index] * sums[dest]
            found.append((index, dest, soft, soft.astype(BF).astype(F32) * prob_grad[index]))
        for index, dest, soft, product in found:
            scores[index] = soft
            deltas[dest] += product
        return carry

    lax.fori_loop(0, edge_count // unroll, delta_step, 0)
    for tile in range(dest_tiles):
        deltas[tile] = head_sum(deltas[tile])

    def grad_step(step, carry):
        found = []
        for part in range(unroll):
            index = step * unroll + part
            _, dest, source, rel, prior = entry(index)
            at = rows_of(dest)
            soft = scores[index]
            score_grad = soft * (prob_grad[index] - deltas[dest])
            prior_now = jnp.sum(score_grad * logits[index], axis=0, keepdims=True)
            logit_grad = (score_grad * (prior * (TILE**-0.5))).astype(BF)
            query_now = mm(logit_grad, stacked(mixed[index]), 1, 0)
            mixed_grad = diagonal(mm(logit_grad, query_ref[at], 0, 0)).astype(BF)
            message_grad = diagonal(mm(soft.astype(BF), grad_ref[at], 0, 0)).astype(BF)
            key_now = mm(mixed_grad, wide[0, rel], 1, 1)
            value_now = mm(message_grad, wide[1, rel], 1, 1)
            score_weight = diagonal(mm(keys[rows_of(source)], mixed_grad, 0, 0))
            message_weight = diagonal(mm(values[rows_of(source)], message_grad, 0, 0))
            found.append(
                (
                    dest,
                    source,
                    rel,
                    prior_now,
                    query_now,
                    key_now,
                    value_now,
                    score_weight,
                    message_weight,
                )
            )
        for dest, source, rel, prior_now, query_now, key_now, value_now, one, two in found:
            prior_out[pl.ds(rel, 1)] += prior_now
            query_acc[dest] += query_now
            key_acc[source] += key_now
            value_acc[source] += value_now
            rel_out[rel] += one
            rel_out[RELS + rel] += two
        return carry

    lax.fori_loop(0, edge_count // unroll, grad_step, 0)
    for tile in range(dest_tiles):
        pack_out[tile * TILE : (tile + 1) * TILE] = query_acc[tile].astype(BF)
        at = own + tile * TILE
        pack_out[at : at + TILE] = key_acc[tile].astype(BF)
        at = 2 * own + tile * TILE
        pack_out[at : at + TILE] = value_acc[tile].astype(BF)
    empty = jnp.zeros((CAP, width), F32)
    for owner in range(halo_out.shape[0]):
        tile, at = dest_tiles + owner * CAP // TILE, owner * CAP % TILE
        halo_out[owner] = jnp.concatenate(
            [
                key_acc[tile, at : at + CAP],
                value_acc[tile, at : at + CAP],
                slot_ref[owner * CAP : (owner + 1) * CAP],
                empty,
            ],
            axis=0,
        ).astype(BF)


def attend(
    queries,
    key_rows,
    value_rows,
    halo_keys,
    halo_values,
    halo_rows,
    grad_output,
    edge_tiles,
    rel_weight,
    rel_prior,
    rel_blocks,
):
    own, width = queries.shape
    halo = halo_keys.shape[0]
    edges = edge_tiles.shape[0]
    dest_tiles = own // TILE
    source_tiles = (own + halo) // TILE
    unroll = 4 if edges % 4 == 0 else 1
    valid = jnp.concatenate([jnp.ones((own,), F32), (halo_rows < own).astype(F32)])
    valid = valid.reshape(source_tiles, 1, TILE)
    valid = jnp.broadcast_to(jnp.concatenate([valid, valid], axis=2), (source_tiles, 8, width))
    slots = jnp.broadcast_to(halo_rows.astype(F32)[:, None], (halo, width))
    per_edge = (edges, TILE, width)
    per_dest = (dest_tiles, TILE, width)
    per_source = (source_tiles, TILE, width)
    return pl.pallas_call(
        functools.partial(attend_kernel, dest_tiles, source_tiles, edges, unroll),
        out_shape=(
            jax.ShapeDtypeStruct((3 * own, width), BF),
            jax.ShapeDtypeStruct((halo // CAP, 4 * CAP, width), BF),
            jax.ShapeDtypeStruct((rel_blocks, TILE, width), F32),
            jax.ShapeDtypeStruct((16, width), F32),
        ),
        in_specs=[SMEM] * 2 + [VMEM] * 9,
        out_specs=(VMEM,) * 4,
        scratch_shapes=[
            pltpu.VMEM((own + halo, width), BF),
            pltpu.VMEM((own + halo, width), BF),
            pltpu.VMEM((2, RELS, width, width), BF),
            pltpu.VMEM(per_edge, BF),
            pltpu.VMEM(per_edge, BF),
            pltpu.VMEM(per_edge, F32),
            pltpu.VMEM(per_edge, F32),
            pltpu.VMEM(per_edge, F32),
            pltpu.VMEM(per_dest, F32),
            pltpu.VMEM(per_dest, F32),
            pltpu.VMEM(per_dest, F32),
            pltpu.VMEM(per_source, F32),
            pltpu.VMEM(per_source, F32),
        ],
        compiler_params=pltpu.CompilerParams(vmem_limit_bytes=48 * 1024 * 1024),
        name="attend",
    )(
        edge_tiles.reshape(-1),
        rel_prior.reshape(-1),
        queries,
        key_rows,
        value_rows,
        halo_keys,
        halo_values,
        grad_output,
        valid,
        slots,
        rel_weight,
    )


def exchange_kernel(
    nodes,
    heads,
    shard,
    pack_ref,
    halo_ref,
    rel_ref,
    prior_ref,
    feats_ref,
    weight_ref,
    types_ref,
    feats_out,
    proj_out,
    rel_out,
    prior_out,
    pack,
    left_in,
    back_in,
    back,
    prior_in,
    rel_send,
    rel_in,
    rel_half,
    rel_half_bf,
    rel_parts,
    feat_acc,
    feat_send,
    feat_in,
    acc,
    part_send,
    part_in,
    halo_sems,
    prior_sems,
    left_sems,
    pack_sems,
    back_sems,
    pair_sems,
    split_sems,
    spread_sems,
    across_sems,
    head_sems,
    part_sems,
):
    lines = nodes // 2
    node = lax.axis_index("nodes")
    head = lax.axis_index("heads")
    line = node // 2
    side = node % 2
    own = types_ref.shape[0]
    width = pack.shape[2]
    slots = CAP * nodes
    half = rel_half.shape[0]
    piece = half // lines
    mesh = pl.DeviceIdType.MESH

    barrier = pltpu.get_barrier_semaphore()
    for step in range(1, nodes):
        peer = (lax.rem(node + step, nodes), head)
        pl.semaphore_signal(barrier, inc=1, device_id=peer, device_id_type=mesh)
    for step in range(1, heads):
        peer = (node, lax.rem(head + step, heads))
        pl.semaphore_signal(barrier, inc=1, device_id=peer, device_id_type=mesh)

    def copy(source, target, sems, index, to_node, to_head=None):
        return pltpu.make_async_remote_copy(
            src_ref=source,
            dst_ref=target,
            send_sem=sems.at[0, index],
            recv_sem=sems.at[1, index],
            device_id=(to_node, head if to_head is None else to_head),
            device_id_type=mesh,
        )

    def at_line(where):
        return where * 2 + side

    def travel(buffer, sems, step, act):
        block = line - step + 1

        @pl.when((line + 1 < lines) & (block >= 0))
        def _():
            here = buffer.at[block]
            act(
                pltpu.make_async_remote_copy(
                    src_ref=here,
                    dst_ref=here,
                    send_sem=sems.at[0, step],
                    recv_sem=sems.at[1, step],
                    device_id=(at_line(line + 1), head),
                    device_id_type=mesh,
                )
            )

        other = line + step - 1

        @pl.when((line >= 1) & (other < lines))
        def _():
            here = buffer.at[other]
            act(
                pltpu.make_async_remote_copy(
                    src_ref=here,
                    dst_ref=here,
                    send_sem=sems.at[2, step],
                    recv_sem=sems.at[3, step],
                    device_id=(at_line(line - 1), head),
                    device_id_type=mesh,
                )
            )

    def landed(buffer, sems, index, step, block):
        here = buffer.at[block]
        pltpu.make_async_remote_copy(
            src_ref=here,
            dst_ref=here,
            send_sem=sems.at[0, step],
            recv_sem=sems.at[index, step],
            device_id=(lax.rem(node + 1, nodes), head),
            device_id_type=mesh,
        ).wait_recv()

    def start(item):
        item.start()

    def wait_send(item):
        item.wait_send()

    pack[line] = pack_ref[...]
    left_in[line] = feats_ref[line]
    back_in[node] = halo_ref[node]
    prior_in[node] = prior_ref[...]
    rel_send[...] = rel_ref[pl.ds(pl.multiple_of((1 - side) * half, 16), half)].astype(BF)
    pl.semaphore_wait(barrier, nodes + heads - 2)

    halo_copies, prior_copies, left_copies = [], [], []
    for step in range(1, nodes):
        to = lax.rem(node + step, nodes)
        halo_copies.append(copy(halo_ref.at[to], back_in.at[node], halo_sems, step, to))
        halo_copies[-1].start()
    pair = copy(rel_send, rel_in, pair_sems, 0, line * 2 + 1 - side)
    pair.start()
    travel(pack, pack_sems, 1, start)
    for step in range(1, lines):
        to = lax.rem(line + step, lines)
        left_copies.append(
            copy(feats_ref.at[to], left_in.at[line], left_sems, step, at_line(to))
        )
        left_copies[-1].start()
    for step in range(1, nodes):
        to = lax.rem(node + step, nodes)
        prior_copies.append(copy(prior_ref, prior_in.at[node], prior_sems, step, to))
        prior_copies[-1].start()

    types = types_ref[...].astype(F32)
    type_masks = [(types == float(kind)).astype(F32).astype(BF) for kind in range(TYPES)]
    for group in range(3):
        rows = pack_ref[group * own : (group + 1) * own]
        total = sum(
            mm(rows * type_masks[kind], weight_ref[group, kind], 1, 1) for kind in range(TYPES)
        )
        if group == 0:
            feat_acc[...] = total
        else:
            feat_acc[...] += total

    for item in halo_copies:
        item.wait_recv()
    returned = back_in[...].astype(F32)
    key_back = returned[:, :CAP].reshape(slots, width).astype(BF)
    value_back = returned[:, CAP : 2 * CAP].reshape(slots, width).astype(BF)
    ids = returned[:, 2 * CAP : 3 * CAP].reshape(slots, width)
    back[line, :slots] = key_back
    back[line, slots : 2 * slots] = value_back
    back[line, 2 * slots :] = ids.astype(BF)
    travel(back, back_sems, 1, start)

    def chosen(found):
        wide = jnp.concatenate([found] * (own // width), axis=1)
        place = lax.broadcasted_iota(jnp.int32, (slots, own), 1).astype(F32)
        return (wide == place).astype(F32).astype(BF)

    pick = chosen(ids)
    feat_back = jnp.zeros((slots, feat_acc.shape[1]), F32)
    for kind in range(TYPES):
        kept = mm(pick, type_masks[kind], 1, 0).astype(BF)
        feat_back += mm(key_back * kept, weight_ref[1, kind], 1, 1)
        feat_back += mm(value_back * kept, weight_ref[2, kind], 1, 1)
    upper = feat_back.astype(BF)
    lower = (feat_back - upper.astype(F32)).astype(BF)
    feat_acc[...] += mm(pick, upper, 0, 0) + mm(pick, lower, 0, 0)
    for index in range(heads):
        feat_send[index] = feat_acc[:, index * width : (index + 1) * width].astype(BF)
    head_copies = []
    for step in range(1, heads):
        to = lax.rem(head + step, heads)
        head_copies.append(copy(feat_send.at[to], feat_in.at[step], head_sems, step, node, to))
        head_copies[-1].start()

    pair.wait_recv()
    own_half = rel_ref[pl.ds(pl.multiple_of(side * half, 16), half)]
    rel_half[...] = own_half + rel_in[...].astype(F32)
    rel_half_bf[...] = rel_half[...].astype(BF)
    split_copies = []
    for step in range(1, lines):
        to = lax.rem(line + step, lines)
        part = rel_half_bf.at[pl.ds(pl.multiple_of(to * piece, 16), piece)]
        split_copies.append(copy(part, rel_parts.at[step], split_sems, step, at_line(to)))
        split_copies[-1].start()

    acc[...] = jnp.zeros_like(acc)

    def gather_step(block):
        rows = left_in[block]
        kinds = rows[2 * shard : 2 * shard + 1].astype(F32)
        feats = rows[: 2 * shard]
        masked = jnp.concatenate(
            [feats * (kinds == float(kind)).astype(F32).astype(BF) for kind in range(TYPES)],
            axis=0,
        )
        right = jnp.concatenate(
            [pack[block, group * own : (group + 1) * own] for group in range(3)], axis=1
        )
        acc[...] += mm(masked, right, 1, 0)
        return masked

    def return_step(block, masked):
        pick_now = chosen(back[block, 2 * slots :].astype(F32))
        taken = mm(masked, pick_now, 1, 1).astype(BF)
        right = jnp.concatenate([back[block, :slots], back[block, slots : 2 * slots]], axis=1)
        acc[:, width:] += mm(taken, right, 1, 0)

    return_step(line, gather_step(line))

    spread_copies, across_copies = [], []

    def send_across(index, slot):
        here = rel_out.at[side, slot]
        across_copies.append(copy(here, here, across_sems, index, line * 2 + 1 - side))
        across_copies[-1].start()

    for item in left_copies:
        item.wait_recv()
    for step in range(1, lines):

        @pl.when(line - step >= 0)
        def _():
            landed(pack, pack_sems, 1, step, line - step)

        @pl.when(line + step < lines)
        def _():
            landed(pack, pack_sems, 3, step, line + step)

        if step + 1 < lines:
            travel(pack, pack_sems, step + 1, start)

        @pl.when(line - step >= 0)
        def _():
            landed(back, back_sems, 1, step, line - step)

        @pl.when(line + step < lines)
        def _():
            landed(back, back_sems, 3, step, line + step)

        if step + 1 < lines:
            travel(back, back_sems, step + 1, start)

        if step == 1:
            for item in split_copies:
                item.wait_recv()
            final = rel_half[pl.ds(pl.multiple_of(line * piece, 16), piece)]
            for index in range(1, lines):
                final = final + rel_parts[index].astype(F32)
            rel_out[side, line] = final.astype(BF)
            for index in range(1, lines):
                to = lax.rem(line + index, lines)
                here = rel_out.at[side, line]
                spread_copies.append(copy(here, here, spread_sems, index, at_line(to)))
                spread_copies[-1].start()
            send_across(0, line)

        @pl.when(line - step >= 0)
        def _():
            return_step(line - step, gather_step(line - step))

        @pl.when(line + step < lines)
        def _():
            return_step(line + step, gather_step(line + step))

    def share(of):
        return [
            acc[pl.ds(pl.multiple_of(kind * 2 * shard + of * shard, 8), shard)]
            for kind in range(TYPES)
        ]

    extra = part_send.shape[0] - TYPES * shard
    tail = [jnp.zeros((extra, acc.shape[1]), F32)] if extra else []
    part_send[...] = jnp.concatenate(share(1 - side) + tail, axis=0).astype(BF)
    part = copy(part_send, part_in, part_sems, 0, line * 2 + 1 - side)
    part.start()

    for index, item in enumerate(spread_copies):
        item.wait_recv()
        send_across(index + 1, lax.rem(line - index - 1 + lines, lines))

    for item in head_copies:
        item.wait_recv()
    mine = feat_acc[:, :width] * (head == 0).astype(F32)
    for index in range(1, heads):
        block = feat_acc[:, index * width : (index + 1) * width]
        mine = mine + block * (head == index).astype(F32)
    for step in range(1, heads):
        mine = mine + feat_in[step].astype(F32)
    feats_out[...] = mine.astype(BF)
    for item in prior_copies:
        item.wait_recv()
    total = prior_in[0]
    for index in range(1, nodes):
        total = total + prior_in[index]
    first = lax.broadcasted_iota(jnp.int32, total.shape, 1) < TILE
    one = jnp.sum(jnp.where(first, total, 0.0), axis=1, keepdims=True)
    two = jnp.sum(jnp.where(first, 0.0, total), axis=1, keepdims=True)
    prior_out[...] = jnp.where(first, one, two)

    part.wait_recv()
    other = part_in[...].astype(F32)
    for kind, rows in enumerate(share(side)):
        rows = rows + other[kind * shard : (kind + 1) * shard]
        for group in range(3):
            proj_out[group, kind] = rows[:, group * width : (group + 1) * width]
    for item in across_copies:
        item.wait_recv()

    sent = halo_copies + prior_copies + left_copies + head_copies + split_copies
    for item in sent + spread_copies + across_copies + [pair, part]:
        item.wait_send()
    for step in range(1, lines):
        travel(pack, pack_sems, step, wait_send)
        travel(back, back_sems, step, wait_send)


def exchange(nodes, heads, pack, halo, rel, prior, feats, weight, types):
    own = types.shape[0]
    width = pack.shape[1]
    lines = nodes // 2
    features = weight.shape[2]
    shard = features // nodes
    half = rel.shape[0] // 2
    piece = half // lines
    slots = CAP * nodes
    part_rows = -(-TYPES * shard // 16) * 16

    def sems(*dims):
        return pltpu.SemaphoreType.DMA(dims)

    return pl.pallas_call(
        functools.partial(exchange_kernel, nodes, heads, shard),
        out_shape=(
            jax.ShapeDtypeStruct((own, width), BF),
            jax.ShapeDtypeStruct((3, TYPES, shard, width), F32),
            jax.ShapeDtypeStruct((2, lines, piece, width), BF),
            jax.ShapeDtypeStruct((16, width), F32),
        ),
        in_specs=[VMEM] * 7,
        out_specs=(VMEM,) * 4,
        scratch_shapes=[
            pltpu.VMEM((lines, 3 * own, width), BF),
            pltpu.VMEM((lines,) + feats.shape[1:], BF),
            pltpu.VMEM((nodes, 4 * CAP, width), BF),
            pltpu.VMEM((lines, 3 * slots, width), BF),
            pltpu.VMEM((nodes, 16, width), F32),
            pltpu.VMEM((half, width), BF),
            pltpu.VMEM((half, width), BF),
            pltpu.VMEM((half, width), F32),
            pltpu.VMEM((half, width), BF),
            pltpu.VMEM((lines, piece, width), BF),
            pltpu.VMEM((own, features), F32),
            pltpu.VMEM((heads, own, width), BF),
            pltpu.VMEM((heads, own, width), BF),
            pltpu.VMEM((TYPES * 2 * shard, 3 * width), F32),
            pltpu.VMEM((part_rows, 3 * width), BF),
            pltpu.VMEM((part_rows, 3 * width), BF),
            sems(2, nodes),
            sems(2, nodes),
            sems(2, lines),
            sems(4, lines),
            sems(4, lines),
            sems(2, 1),
            sems(2, lines),
            sems(2, lines),
            sems(2, lines),
            sems(2, heads),
            sems(2, 1),
        ],
        compiler_params=pltpu.CompilerParams(
            collective_id=0, has_side_effects=True, vmem_limit_bytes=56 * 1024 * 1024
        ),
        name="exchange",
    )(pack, halo, rel, prior, feats, weight, types)


def per_device(
    nodes,
    heads,
    node_feats,
    node_types,
    queries,
    key_rows,
    value_rows,
    halo_keys,
    halo_values,
    halo_rows,
    edge_tiles,
    grad_output,
    proj_weight,
    rel_weight,
    rel_prior,
):
    own, features = node_feats.shape
    width = queries.shape[1]
    lines = nodes // 2
    shard = features // nodes
    piece = -(-2 * RELS * TILE // nodes // 16) * 16
    rel_rows = max(piece * nodes, 2 * RELS * TILE)
    pack, halo, rel, prior = attend(
        queries,
        key_rows,
        value_rows,
        halo_keys,
        halo_values,
        halo_rows,
        grad_output,
        edge_tiles,
        rel_weight,
        rel_prior,
        rel_rows // TILE,
    )
    kinds = jnp.broadcast_to(node_types.astype(BF)[None, None, :], (lines, 16, own))
    feats = node_feats.T.reshape(lines, 2 * shard, own)
    feats = jnp.concatenate([feats, kinds], axis=1)
    types = jnp.broadcast_to(node_types[:, None], (own, width))
    grad_feats, proj, rel, prior = exchange(
        nodes,
        heads,
        pack,
        halo,
        rel.reshape(rel_rows, width),
        prior,
        feats,
        proj_weight,
        types,
    )
    grad_proj = jnp.transpose(proj, (2, 0, 1, 3))
    rel = rel.reshape(rel_rows, width)[: 2 * RELS * TILE].astype(F32)
    grad_rel = jnp.transpose(rel.reshape(2, RELS, TILE, 2, TILE), (0, 1, 3, 2, 4))
    grad_prior = prior[:RELS, ::TILE]
    return (grad_feats, grad_proj, grad_rel, grad_prior)


def solution(mesh):
    return jax.shard_map(
        functools.partial(per_device, mesh.shape["nodes"], mesh.shape["heads"]),
        mesh=mesh,
        in_specs=(
            P("nodes", None),
            P("nodes"),
            P("nodes", "heads"),
            P("nodes", "heads"),
            P("nodes", "heads"),
            P("nodes", "heads"),
            P("nodes", "heads"),
            P("nodes"),
            P("nodes", None),
            P("nodes", "heads"),
            P(None, None, None, "heads"),
            P(None, None, "heads", None, None),
            P(None, "heads"),
        ),
        out_specs=(
            P("nodes", "heads"),
            P("nodes", None, None, "heads"),
            P(None, None, "heads", None, None),
            P(None, "heads"),
        ),
        check_vma=False,
    )
```

```python
import functools

import jax
import jax.numpy as jnp
from jax import lax
from jax.experimental import pallas as pl
from jax.experimental.pallas import tpu as pltpu
from jax.sharding import PartitionSpec as P

TYPES = 5
RELS = 15
TILE = 64
CAP = 8
BF = jnp.bfloat16
F32 = jnp.float32
VMEM = pl.BlockSpec(memory_space=pltpu.VMEM)
SMEM = pl.BlockSpec(memory_space=pltpu.SMEM)
HBM = pl.BlockSpec(memory_space=pltpu.HBM)


def mm(left, right, left_dim, right_dim):
    return lax.dot_general(
        left, right, (((left_dim,), (right_dim,)), ((), ())), preferred_element_type=F32
    )


def attend_kernel(
    dest_tiles,
    source_tiles,
    edge_count,
    unroll,
    edge_ref,
    prior_ref,
    slot_ref,
    query_hbm,
    key_hbm,
    value_hbm,
    halo_key_hbm,
    halo_value_hbm,
    grad_hbm,
    weight_hbm,
    pack_out,
    halo_out,
    rel_out,
    prior_out,
    query_ref,
    grad_ref,
    weight_ref,
    keys,
    values,
    wide,
    mixed,
    message,
    logits,
    scores,
    prob_grad,
    sums,
    deltas,
    query_acc,
    key_acc,
    value_acc,
    valid_ref,
    load_sems,
):
    own = dest_tiles * TILE
    halo = (source_tiles - dest_tiles) * TILE
    width = 2 * TILE
    loads = [
        pltpu.make_async_copy(source, target, load_sems.at[index])
        for index, (source, target) in enumerate(
            (
                (weight_hbm, weight_ref),
                (key_hbm, keys.at[:own]),
                (halo_key_hbm, keys.at[own:]),
                (value_hbm, values.at[:own]),
                (halo_value_hbm, values.at[own:]),
                (query_hbm, query_ref),
                (grad_hbm, grad_ref),
            )
        )
    ]
    for load in loads:
        load.start()
    for ref in (sums, deltas, query_acc, key_acc, value_acc, rel_out, prior_out):
        ref[...] = jnp.zeros_like(ref)
    lane = lax.broadcasted_iota(jnp.int32, (8, width), 1) % TILE
    for tile in range(dest_tiles):
        valid_ref[tile] = jnp.ones((8, width), F32)
    for tile in range(halo // TILE):
        found = jnp.zeros((8, width), F32)
        for index in range(TILE):
            inside = jnp.where(slot_ref[tile * TILE + index] < own, 1.0, 0.0)
            found = jnp.where(lane == index, inside, found)
        valid_ref[dest_tiles + tile] = found
    for load in loads:
        load.wait()
    blank = jnp.zeros((TILE, TILE), BF)
    for side in range(2):
        for rel in range(RELS):
            wide[side, rel] = jnp.concatenate(
                [
                    jnp.concatenate([weight_ref[side, rel, 0], blank], axis=1),
                    jnp.concatenate([blank, weight_ref[side, rel, 1]], axis=1),
                ],
                axis=0,
            )
    first = lax.broadcasted_iota(jnp.int32, (TILE, width), 1) < TILE
    first_row = lax.broadcasted_iota(jnp.int32, (1, width), 1) < TILE
    low = first.astype(F32).astype(BF)
    high = (1.0 - first.astype(F32)).astype(BF)

    def stacked(both):
        return jnp.concatenate([both * low, both * high], axis=0)

    def diagonal(square):
        return jnp.where(first, square[:TILE], square[TILE:])

    def head_sum(total):
        left = jnp.sum(jnp.where(first, total, 0.0), axis=1, keepdims=True)
        right = jnp.sum(jnp.where(first, 0.0, total), axis=1, keepdims=True)
        return jnp.where(first, left, right)

    def entry(index):
        target = edge_ref[index, 0]
        live = target < dest_tiles
        dest = jnp.minimum(target, dest_tiles - 1)
        source = edge_ref[index, 1]
        rel = edge_ref[index, 2]
        prior = jnp.where(first_row, prior_ref[rel, 0], prior_ref[rel, 1])
        return live, dest, source, rel, prior

    def rows_of(tile):
        return pl.ds(pl.multiple_of(tile * TILE, TILE), TILE)

    def score_step(step, carry):
        found = []
        for part in range(unroll):
            index = step * unroll + part
            live, dest, source, rel, prior = entry(index)
            at = rows_of(dest)
            mixed_now = mm(keys[rows_of(source)], wide[0, rel], 1, 0).astype(BF)
            message_now = mm(values[rows_of(source)], wide[1, rel], 1, 0).astype(BF)
            logit = mm(query_ref[at], stacked(mixed_now), 1, 1) * (TILE**-0.5)
            grad = mm(grad_ref[at], stacked(message_now), 1, 1)
            keep = valid_ref[source][:1] * jnp.where(live, 1.0, 0.0)
            score = jnp.where(keep > 0.0, jnp.exp(logit * prior), 0.0)
            found.append((index, dest, mixed_now, message_now, logit, grad, score))
        for index, dest, mixed_now, message_now, logit, grad, score in found:
            mixed[index] = mixed_now
            message[index] = message_now
            logits[index] = logit
            prob_grad[index] = grad
            scores[index] = score
            sums[dest] += score
        return carry

    lax.fori_loop(0, edge_count // unroll, score_step, 0)
    for tile in range(dest_tiles):
        sums[tile] = 1.0 / head_sum(sums[tile])

    def delta_step(step, carry):
        found = []
        for part in range(unroll):
            index = step * unroll + part
            _, dest, _, _, _ = entry(index)
            soft = scores[index] * sums[dest]
            found.append((index, dest, soft, soft.astype(BF).astype(F32) * prob_grad[index]))
        for index, dest, soft, product in found:
            scores[index] = soft
            deltas[dest] += product
        return carry

    lax.fori_loop(0, edge_count // unroll, delta_step, 0)
    for tile in range(dest_tiles):
        deltas[tile] = head_sum(deltas[tile])

    def grad_step(step, carry):
        found = []
        for part in range(unroll):
            index = step * unroll + part
            _, dest, source, rel, prior = entry(index)
            at = rows_of(dest)
            soft = scores[index]
            score_grad = soft * (prob_grad[index] - deltas[dest])
            prior_now = jnp.sum(score_grad * logits[index], axis=0, keepdims=True)
            logit_grad = (score_grad * (prior * (TILE**-0.5))).astype(BF)
            query_now = mm(logit_grad, stacked(mixed[index]), 1, 0)
            mixed_grad = diagonal(mm(logit_grad, query_ref[at], 0, 0)).astype(BF)
            message_grad = diagonal(mm(soft.astype(BF), grad_ref[at], 0, 0)).astype(BF)
            key_now = mm(mixed_grad, wide[0, rel], 1, 1)
            value_now = mm(message_grad, wide[1, rel], 1, 1)
            score_weight = diagonal(mm(keys[rows_of(source)], mixed_grad, 0, 0))
            message_weight = diagonal(mm(values[rows_of(source)], message_grad, 0, 0))
            found.append(
                (
                    dest,
                    source,
                    rel,
                    prior_now,
                    query_now,
                    key_now,
                    value_now,
                    score_weight,
                    message_weight,
                )
            )
        for dest, source, rel, prior_now, query_now, key_now, value_now, one, two in found:
            prior_out[pl.ds(rel, 1)] += prior_now
            query_acc[dest] += query_now
            key_acc[source] += key_now
            value_acc[source] += value_now
            rel_out[rel] += one
            rel_out[RELS + rel] += two
        return carry

    lax.fori_loop(0, edge_count // unroll, grad_step, 0)
    for tile in range(dest_tiles):
        pack_out[tile * TILE : (tile + 1) * TILE] = query_acc[tile].astype(BF)
        at = own + tile * TILE
        pack_out[at : at + TILE] = key_acc[tile].astype(BF)
        at = 2 * own + tile * TILE
        pack_out[at : at + TILE] = value_acc[tile].astype(BF)
    empty = jnp.zeros((CAP, width), F32)
    slot_row = lax.broadcasted_iota(jnp.int32, (CAP, width), 0)
    for owner in range(halo_out.shape[0]):
        rows = empty
        for index in range(CAP):
            row = slot_ref[owner * CAP + index].astype(F32)
            rows = jnp.where(slot_row == index, row, rows)
        tile, at = dest_tiles + owner * CAP // TILE, owner * CAP % TILE
        halo_out[owner] = jnp.concatenate(
            [
                key_acc[tile, at : at + CAP],
                value_acc[tile, at : at + CAP],
                rows,
                empty,
            ],
            axis=0,
        ).astype(BF)


def attend(
    queries,
    key_rows,
    value_rows,
    halo_keys,
    halo_values,
    halo_rows,
    grad_output,
    edge_tiles,
    rel_weight,
    rel_prior,
    rel_blocks,
):
    own, width = queries.shape
    halo = halo_keys.shape[0]
    edges = edge_tiles.shape[0]
    dest_tiles = own // TILE
    source_tiles = (own + halo) // TILE
    unroll = 4 if edges % 4 == 0 else 1
    per_edge = (edges, TILE, width)
    per_dest = (dest_tiles, TILE, width)
    per_source = (source_tiles, TILE, width)
    return pl.pallas_call(
        functools.partial(attend_kernel, dest_tiles, source_tiles, edges, unroll),
        out_shape=(
            jax.ShapeDtypeStruct((3 * own, width), BF),
            jax.ShapeDtypeStruct((halo // CAP, 4 * CAP, width), BF),
            jax.ShapeDtypeStruct((rel_blocks, TILE, width), F32),
            jax.ShapeDtypeStruct((16, width), F32),
        ),
        in_specs=[SMEM] * 3 + [HBM] * 7,
        out_specs=(VMEM,) * 4,
        scratch_shapes=[
            pltpu.VMEM((own, width), BF),
            pltpu.VMEM((own, width), BF),
            pltpu.VMEM(rel_weight.shape, BF),
            pltpu.VMEM((own + halo, width), BF),
            pltpu.VMEM((own + halo, width), BF),
            pltpu.VMEM((2, RELS, width, width), BF),
            pltpu.VMEM(per_edge, BF),
            pltpu.VMEM(per_edge, BF),
            pltpu.VMEM(per_edge, F32),
            pltpu.VMEM(per_edge, F32),
            pltpu.VMEM(per_edge, F32),
            pltpu.VMEM(per_dest, F32),
            pltpu.VMEM(per_dest, F32),
            pltpu.VMEM(per_dest, F32),
            pltpu.VMEM(per_source, F32),
            pltpu.VMEM(per_source, F32),
            pltpu.VMEM((source_tiles, 8, width), F32),
            pltpu.SemaphoreType.DMA((7,)),
        ],
        compiler_params=pltpu.CompilerParams(vmem_limit_bytes=60 * 1024 * 1024),
        name="attend",
    )(
        edge_tiles,
        rel_prior,
        halo_rows,
        queries,
        key_rows,
        value_rows,
        halo_keys,
        halo_values,
        grad_output,
        rel_weight,
    )


def exchange_kernel(
    nodes,
    heads,
    shard,
    pack_ref,
    halo_ref,
    rel_ref,
    prior_ref,
    feats_ref,
    weight_hbm,
    types_ref,
    feats_out,
    proj_out,
    rel_out,
    prior_out,
    pack,
    left_in,
    back_in,
    back,
    prior_in,
    rel_send,
    rel_in,
    rel_half,
    rel_half_bf,
    rel_parts,
    feat_acc,
    feat_send,
    feat_in,
    acc,
    part_send,
    part_in,
    weight_ref,
    local_sems,
    halo_sems,
    prior_sems,
    left_sems,
    share_sems,
    pack_sems,
    back_sems,
    pair_sems,
    split_sems,
    spread_sems,
    across_sems,
    head_sems,
    part_sems,
):
    lines = nodes // 2
    node = lax.axis_index("nodes")
    head = lax.axis_index("heads")
    line = node // 2
    side = node % 2
    own = feats_ref.shape[3]
    cuts = feats_ref.shape[1]
    width = pack.shape[2]
    slots = CAP * nodes
    half = rel_half.shape[0]
    piece = half // lines
    mesh = pl.DeviceIdType.MESH

    barrier = pltpu.get_barrier_semaphore()
    for step in range(1, nodes):
        peer = (lax.rem(node + step, nodes), head)
        pl.semaphore_signal(barrier, inc=1, device_id=peer, device_id_type=mesh)
    for step in range(1, heads):
        peer = (node, lax.rem(head + step, heads))
        pl.semaphore_signal(barrier, inc=1, device_id=peer, device_id_type=mesh)

    def copy(source, target, sems, index, to_node, to_head=None):
        return pltpu.make_async_remote_copy(
            src_ref=source,
            dst_ref=target,
            send_sem=sems.at[0, index],
            recv_sem=sems.at[1, index],
            device_id=(to_node, head if to_head is None else to_head),
            device_id_type=mesh,
        )

    def at_line(where):
        return where * 2 + side

    def travel(buffer, sems, step, act):
        block = line - step + 1

        @pl.when((line + 1 < lines) & (block >= 0))
        def _():
            here = buffer.at[block]
            act(
                pltpu.make_async_remote_copy(
                    src_ref=here,
                    dst_ref=here,
                    send_sem=sems.at[0, step],
                    recv_sem=sems.at[1, step],
                    device_id=(at_line(line + 1), head),
                    device_id_type=mesh,
                )
            )

        other = line + step - 1

        @pl.when((line >= 1) & (other < lines))
        def _():
            here = buffer.at[other]
            act(
                pltpu.make_async_remote_copy(
                    src_ref=here,
                    dst_ref=here,
                    send_sem=sems.at[2, step],
                    recv_sem=sems.at[3, step],
                    device_id=(at_line(line - 1), head),
                    device_id_type=mesh,
                )
            )

    def landed(buffer, sems, index, step, block):
        here = buffer.at[block]
        pltpu.make_async_remote_copy(
            src_ref=here,
            dst_ref=here,
            send_sem=sems.at[0, step],
            recv_sem=sems.at[index, step],
            device_id=(lax.rem(node + 1, nodes), head),
            device_id_type=mesh,
        ).wait_recv()

    def start(item):
        item.start()

    def wait_send(item):
        item.wait_send()

    loads = [
        pltpu.make_async_copy(weight_hbm, weight_ref, local_sems.at[0]),
        pltpu.make_async_copy(feats_ref.at[line], left_in.at[line], local_sems.at[1]),
    ]
    for load in loads:
        load.start()
    pack[line, : 3 * own] = pack_ref[...]
    pack[line, 3 * own :] = types_ref[...]
    back_in[node] = halo_ref[node]
    prior_in[node] = prior_ref[...]
    rel_send[...] = rel_ref[pl.ds(pl.multiple_of((1 - side) * half, 16), half)].astype(BF)
    pl.semaphore_wait(barrier, nodes + heads - 2)

    halo_copies, prior_copies, left_copies = [], [], []
    for step in range(1, nodes):
        to = lax.rem(node + step, nodes)
        halo_copies.append(copy(halo_ref.at[to], back_in.at[node], halo_sems, step, to))
        halo_copies[-1].start()
    pair = copy(rel_send, rel_in, pair_sems, 0, line * 2 + 1 - side)
    pair.start()
    travel(pack, pack_sems, 1, start)
    for step in range(1, lines):
        to = lax.rem(line + step, lines)
        here, there = feats_ref.at[to], left_in.at[line]
        if cuts > 1:
            here, there = here.at[head], there.at[head]
        left_copies.append(copy(here, there, left_sems, step, at_line(to)))
        left_copies[-1].start()
    for step in range(1, nodes):
        to = lax.rem(node + step, nodes)
        prior_copies.append(copy(prior_ref, prior_in.at[node], prior_sems, step, to))
        prior_copies[-1].start()

    def kinds_of(block):
        found = pack[block, 3 * own :].astype(F32)
        return jnp.concatenate([found[row : row + 1] for row in range(own // width)], axis=1)

    square = (own, own)
    even = lax.broadcasted_iota(jnp.int32, square, 0) == lax.broadcasted_iota(
        jnp.int32, square, 1
    )
    spread = jnp.where(even, kinds_of(line), 0.0).astype(BF)
    types = mm(spread, jnp.ones((own, width), BF), 1, 0)
    for load in loads:
        load.wait()
    type_masks = [(types == float(kind)).astype(F32).astype(BF) for kind in range(TYPES)]
    for group in range(3):
        rows = pack_ref[group * own : (group + 1) * own]
        total = sum(
            mm(rows * type_masks[kind], weight_ref[group, kind], 1, 1) for kind in range(TYPES)
        )
        if group == 0:
            feat_acc[...] = total
        else:
            feat_acc[...] += total

    for item in halo_copies:
        item.wait_recv()
    returned = back_in[...].astype(F32)
    key_back = returned[:, :CAP].reshape(slots, width).astype(BF)
    value_back = returned[:, CAP : 2 * CAP].reshape(slots, width).astype(BF)
    ids = returned[:, 2 * CAP : 3 * CAP].reshape(slots, width)
    back[line, :slots] = key_back
    back[line, slots : 2 * slots] = value_back
    back[line, 2 * slots :] = ids.astype(BF)
    travel(back, back_sems, 1, start)

    def chosen(found):
        wide = jnp.concatenate([found] * (own // width), axis=1)
        place = lax.broadcasted_iota(jnp.int32, (slots, own), 1).astype(F32)
        return (wide == place).astype(F32).astype(BF)

    pick = chosen(ids)
    feat_back = jnp.zeros((slots, feat_acc.shape[1]), F32)
    for kind in range(TYPES):
        kept = mm(pick, type_masks[kind], 1, 0).astype(BF)
        feat_back += mm(key_back * kept, weight_ref[1, kind], 1, 1)
        feat_back += mm(value_back * kept, weight_ref[2, kind], 1, 1)
    upper = feat_back.astype(BF)
    lower = (feat_back - upper.astype(F32)).astype(BF)
    feat_acc[...] += mm(pick, upper, 0, 0) + mm(pick, lower, 0, 0)
    for index in range(heads):
        feat_send[index] = feat_acc[:, index * width : (index + 1) * width].astype(BF)
    head_copies = []
    for step in range(1, heads):
        to = lax.rem(head + step, heads)
        head_copies.append(copy(feat_send.at[to], feat_in.at[step], head_sems, step, node, to))
        head_copies[-1].start()

    share_copies = []
    for step, item in enumerate(left_copies, 1):
        item.wait_recv()
        if cuts > 1:
            here = left_in.at[lax.rem(line - step + lines, lines), head]
            for other in range(1, heads):
                to = lax.rem(head + other, heads)
                index = step * heads + other
                share_copies.append(copy(here, here, share_sems, index, node, to))
                share_copies[-1].start()

    pair.wait_recv()
    own_half = rel_ref[pl.ds(pl.multiple_of(side * half, 16), half)]
    rel_half[...] = own_half + rel_in[...].astype(F32)
    rel_half_bf[...] = rel_half[...].astype(BF)
    split_copies = []
    for step in range(1, lines):
        to = lax.rem(line + step, lines)
        part = rel_half_bf.at[pl.ds(pl.multiple_of(to * piece, 16), piece)]
        split_copies.append(copy(part, rel_parts.at[step], split_sems, step, at_line(to)))
        split_copies[-1].start()

    acc[...] = jnp.zeros_like(acc)

    def gather_step(block):
        feats = left_in[block].reshape(2 * shard, own)
        kinds = kinds_of(block)
        masked = jnp.concatenate(
            [feats * (kinds == float(kind)).astype(F32).astype(BF) for kind in range(TYPES)],
            axis=0,
        )
        right = jnp.concatenate(
            [pack[block, group * own : (group + 1) * own] for group in range(3)], axis=1
        )
        acc[...] += mm(masked, right, 1, 0)
        return masked

    def return_step(block, masked):
        pick_now = chosen(back[block, 2 * slots :].astype(F32))
        taken = mm(masked, pick_now, 1, 1).astype(BF)
        right = jnp.concatenate([back[block, :slots], back[block, slots : 2 * slots]], axis=1)
        acc[:, width:] += mm(taken, right, 1, 0)

    return_step(line, gather_step(line))

    def across(slot):
        here = rel_out.at[side, slot]
        return copy(here, here, across_sems, slot, line * 2 + 1 - side)

    def send_across(slot):
        across(slot).start()

    for item in share_copies:
        item.wait_recv()
    for step in range(1, lines):

        @pl.when(line - step >= 0)
        def _():
            landed(pack, pack_sems, 1, step, line - step)

        @pl.when(line + step < lines)
        def _():
            landed(pack, pack_sems, 3, step, line + step)

        if step + 1 < lines:
            travel(pack, pack_sems, step + 1, start)

        @pl.when(line - step >= 0)
        def _():
            landed(back, back_sems, 1, step, line - step)

        @pl.when(line + step < lines)
        def _():
            landed(back, back_sems, 3, step, line + step)

        if step + 1 < lines:
            travel(back, back_sems, step + 1, start)

        if step == 1:
            for item in split_copies:
                item.wait_recv()
            final = rel_half[pl.ds(pl.multiple_of(line * piece, 16), piece)]
            for index in range(1, lines):
                final = final + rel_parts[index].astype(F32)
            rel_out[side, line] = final.astype(BF)
            travel(rel_out.at[side], spread_sems, 1, start)
            send_across(line)

        @pl.when(line - step >= 0)
        def _():
            return_step(line - step, gather_step(line - step))

        @pl.when(line + step < lines)
        def _():
            return_step(line + step, gather_step(line + step))

    def share(of):
        return [
            acc[pl.ds(pl.multiple_of(kind * 2 * shard + of * shard, 8), shard)]
            for kind in range(TYPES)
        ]

    extra = part_send.shape[0] - TYPES * shard
    tail = [jnp.zeros((extra, acc.shape[1]), F32)] if extra else []
    part_send[...] = jnp.concatenate(share(1 - side) + tail, axis=0).astype(BF)
    part = copy(part_send, part_in, part_sems, 0, line * 2 + 1 - side)
    part.start()

    for step in range(1, lines):
        behind, ahead = line - step, line + step

        @pl.when(behind >= 0)
        def _():
            landed(rel_out.at[side], spread_sems, 1, step, behind)

        @pl.when(ahead < lines)
        def _():
            landed(rel_out.at[side], spread_sems, 3, step, ahead)

        if step + 1 < lines:
            travel(rel_out.at[side], spread_sems, step + 1, start)

        @pl.when(behind >= 0)
        def _():
            send_across(behind)

        @pl.when(ahead < lines)
        def _():
            send_across(ahead)

    for item in head_copies:
        item.wait_recv()
    mine = feat_acc[:, :width] * (head == 0).astype(F32)
    for index in range(1, heads):
        block = feat_acc[:, index * width : (index + 1) * width]
        mine = mine + block * (head == index).astype(F32)
    for step in range(1, heads):
        mine = mine + feat_in[step].astype(F32)
    feats_out[...] = mine.astype(BF)
    for item in prior_copies:
        item.wait_recv()
    total = prior_in[0]
    for index in range(1, nodes):
        total = total + prior_in[index]
    first = lax.broadcasted_iota(jnp.int32, total.shape, 1) < TILE
    one = jnp.sum(jnp.where(first, total, 0.0), axis=1, keepdims=True)
    two = jnp.sum(jnp.where(first, 0.0, total), axis=1, keepdims=True)
    prior_out[...] = jnp.where(first, one, two)

    part.wait_recv()
    other = part_in[...].astype(F32)
    for kind, rows in enumerate(share(side)):
        rows = rows + other[kind * shard : (kind + 1) * shard]
        for group in range(3):
            proj_out[group, kind] = rows[:, group * width : (group + 1) * width]
    for slot in range(lines):
        across(slot).wait()

    sent = halo_copies + prior_copies + left_copies + head_copies + split_copies
    for item in sent + share_copies + [pair, part]:
        item.wait_send()
    for step in range(1, lines):
        travel(pack, pack_sems, step, wait_send)
        travel(back, back_sems, step, wait_send)
        travel(rel_out.at[side], spread_sems, step, wait_send)


def exchange(nodes, heads, pack, halo, rel, prior, feats, weight, types):
    own = feats.shape[3]
    width = pack.shape[1]
    lines = nodes // 2
    features = weight.shape[2]
    shard = features // nodes
    half = rel.shape[0] // 2
    piece = half // lines
    slots = CAP * nodes
    part_rows = -(-TYPES * shard // 16) * 16

    def sems(*dims):
        return pltpu.SemaphoreType.DMA(dims)

    return pl.pallas_call(
        functools.partial(exchange_kernel, nodes, heads, shard),
        out_shape=(
            jax.ShapeDtypeStruct((own, width), BF),
            jax.ShapeDtypeStruct((3, TYPES, shard, width), F32),
            jax.ShapeDtypeStruct((2, lines, piece, width), BF),
            jax.ShapeDtypeStruct((16, width), F32),
        ),
        in_specs=[VMEM] * 4 + [HBM] * 2 + [VMEM],
        out_specs=(VMEM,) * 4,
        scratch_shapes=[
            pltpu.VMEM((lines, 3 * own + 16, width), BF),
            pltpu.VMEM((lines,) + feats.shape[1:], BF),
            pltpu.VMEM((nodes, 4 * CAP, width), BF),
            pltpu.VMEM((lines, 3 * slots, width), BF),
            pltpu.VMEM((nodes, 16, width), F32),
            pltpu.VMEM((half, width), BF),
            pltpu.VMEM((half, width), BF),
            pltpu.VMEM((half, width), F32),
            pltpu.VMEM((half, width), BF),
            pltpu.VMEM((lines, piece, width), BF),
            pltpu.VMEM((own, features), F32),
            pltpu.VMEM((heads, own, width), BF),
            pltpu.VMEM((heads, own, width), BF),
            pltpu.VMEM((TYPES * 2 * shard, 3 * width), F32),
            pltpu.VMEM((part_rows, 3 * width), BF),
            pltpu.VMEM((part_rows, 3 * width), BF),
            pltpu.VMEM(weight.shape, BF),
            sems(2),
            sems(2, nodes),
            sems(2, nodes),
            sems(2, lines),
            sems(2, lines * heads),
            sems(4, lines),
            sems(4, lines),
            sems(2, 1),
            sems(2, lines),
            sems(4, lines),
            sems(2, lines),
            sems(2, heads),
            sems(2, 1),
        ],
        compiler_params=pltpu.CompilerParams(
            collective_id=0, has_side_effects=True, vmem_limit_bytes=60 * 1024 * 1024
        ),
        name="exchange",
    )(pack, halo, rel, prior, feats, weight, types)


def per_device(
    nodes,
    heads,
    node_feats,
    node_types,
    queries,
    key_rows,
    value_rows,
    halo_keys,
    halo_values,
    halo_rows,
    edge_tiles,
    grad_output,
    proj_weight,
    rel_weight,
    rel_prior,
):
    own, features = node_feats.shape
    width = queries.shape[1]
    lines = nodes // 2
    shard = features // nodes
    piece = -(-2 * RELS * TILE // nodes // 16) * 16
    rel_rows = max(piece * nodes, 2 * RELS * TILE)
    pack, halo, rel, prior = attend(
        queries,
        key_rows,
        value_rows,
        halo_keys,
        halo_values,
        halo_rows,
        grad_output,
        edge_tiles,
        rel_weight,
        rel_prior,
        rel_rows // TILE,
    )
    cuts = heads if 2 * shard % (16 * heads) == 0 else 1
    feats = node_feats.T.reshape(lines, cuts, 2 * shard // cuts, own)
    types = node_types.astype(BF).reshape(own // width, width)
    types = jnp.pad(types, ((0, 16 - own // width), (0, 0)))
    grad_feats, proj, rel, prior = exchange(
        nodes,
        heads,
        pack,
        halo,
        rel.reshape(rel_rows, width),
        prior,
        feats,
        proj_weight,
        types,
    )
    grad_proj = jnp.transpose(proj, (2, 0, 1, 3))
    rel = rel.reshape(rel_rows, width)[: 2 * RELS * TILE].astype(F32)
    grad_rel = jnp.transpose(rel.reshape(2, RELS, TILE, 2, TILE), (0, 1, 3, 2, 4))
    grad_prior = prior[:RELS, ::TILE]
    return (grad_feats, grad_proj, grad_rel, grad_prior)


def solution(mesh):
    return jax.shard_map(
        functools.partial(per_device, mesh.shape["nodes"], mesh.shape["heads"]),
        mesh=mesh,
        in_specs=(
            P("nodes", None),
            P("nodes"),
            P("nodes", "heads"),
            P("nodes", "heads"),
            P("nodes", "heads"),
            P("nodes", "heads"),
            P("nodes", "heads"),
            P("nodes"),
            P("nodes", None),
            P("nodes", "heads"),
            P(None, None, None, "heads"),
            P(None, None, "heads", None, None),
            P(None, "heads"),
        ),
        out_specs=(
            P("nodes", "heads"),
            P("nodes", None, None, "heads"),
            P(None, None, "heads", None, None),
            P(None, "heads"),
        ),
        check_vma=False,
    )
```

```python
import functools

import jax
import jax.numpy as jnp
from jax import lax
from jax.experimental import pallas as pl
from jax.experimental.pallas import tpu as pltpu
from jax.sharding import PartitionSpec as P

TYPES = 5
RELS = 15
TILE = 64
CAP = 8
BF = jnp.bfloat16
F32 = jnp.float32
VMEM = pl.BlockSpec(memory_space=pltpu.VMEM)
SMEM = pl.BlockSpec(memory_space=pltpu.SMEM)
HBM = pl.BlockSpec(memory_space=pltpu.HBM)


def mm(left, right, left_dim, right_dim):
    return lax.dot_general(
        left, right, (((left_dim,), (right_dim,)), ((), ())), preferred_element_type=F32
    )


def attend_kernel(
    dest_tiles,
    source_tiles,
    edge_count,
    unroll,
    edge_ref,
    prior_ref,
    slot_ref,
    query_hbm,
    key_hbm,
    value_hbm,
    halo_key_hbm,
    halo_value_hbm,
    grad_hbm,
    weight_hbm,
    pack_out,
    halo_out,
    rel_out,
    prior_out,
    query_ref,
    grad_ref,
    weight_ref,
    keys,
    values,
    wide,
    mixed,
    message,
    logits,
    scores,
    prob_grad,
    sums,
    deltas,
    query_acc,
    key_acc,
    value_acc,
    valid_ref,
    load_sems,
):
    own = dest_tiles * TILE
    halo = (source_tiles - dest_tiles) * TILE
    width = 2 * TILE
    loads = [
        pltpu.make_async_copy(source, target, load_sems.at[index])
        for index, (source, target) in enumerate(
            (
                (weight_hbm, weight_ref),
                (key_hbm, keys.at[:own]),
                (halo_key_hbm, keys.at[own:]),
                (value_hbm, values.at[:own]),
                (halo_value_hbm, values.at[own:]),
                (query_hbm, query_ref),
                (grad_hbm, grad_ref),
            )
        )
    ]
    for load in loads:
        load.start()
    for ref in (sums, deltas, query_acc, key_acc, value_acc, rel_out, prior_out):
        ref[...] = jnp.zeros_like(ref)
    lane = lax.broadcasted_iota(jnp.int32, (8, width), 1) % TILE
    for tile in range(dest_tiles):
        valid_ref[tile] = jnp.ones((8, width), F32)
    for tile in range(halo // TILE):
        found = jnp.zeros((8, width), F32)
        for index in range(TILE):
            inside = jnp.where(slot_ref[tile * TILE + index] < own, 1.0, 0.0)
            found = jnp.where(lane == index, inside, found)
        valid_ref[dest_tiles + tile] = found
    for load in loads:
        load.wait()
    blank = jnp.zeros((TILE, TILE), BF)
    for side in range(2):
        for rel in range(RELS):
            wide[side, rel] = jnp.concatenate(
                [
                    jnp.concatenate([weight_ref[side, rel, 0], blank], axis=1),
                    jnp.concatenate([blank, weight_ref[side, rel, 1]], axis=1),
                ],
                axis=0,
            )
    first = lax.broadcasted_iota(jnp.int32, (TILE, width), 1) < TILE
    first_row = lax.broadcasted_iota(jnp.int32, (1, width), 1) < TILE
    low = first.astype(F32).astype(BF)
    high = (1.0 - first.astype(F32)).astype(BF)

    def stacked(both):
        return jnp.concatenate([both * low, both * high], axis=0)

    def diagonal(square):
        return jnp.where(first, square[:TILE], square[TILE:])

    def head_sum(total):
        left = jnp.sum(jnp.where(first, total, 0.0), axis=1, keepdims=True)
        right = jnp.sum(jnp.where(first, 0.0, total), axis=1, keepdims=True)
        return jnp.where(first, left, right)

    def entry(index):
        target = edge_ref[0, index]
        live = target < dest_tiles
        dest = jnp.minimum(target, dest_tiles - 1)
        source = edge_ref[1, index]
        rel = edge_ref[2, index]
        prior = jnp.where(first_row, prior_ref[0, rel], prior_ref[1, rel])
        return live, dest, source, rel, prior

    def rows_of(tile):
        return pl.ds(pl.multiple_of(tile * TILE, TILE), TILE)

    def score_step(step, carry):
        found = []
        for part in range(unroll):
            index = step * unroll + part
            live, dest, source, rel, prior = entry(index)
            at = rows_of(dest)
            mixed_now = mm(keys[rows_of(source)], wide[0, rel], 1, 0).astype(BF)
            message_now = mm(values[rows_of(source)], wide[1, rel], 1, 0).astype(BF)
            logit = mm(query_ref[at], stacked(mixed_now), 1, 1) * (TILE**-0.5)
            grad = mm(grad_ref[at], stacked(message_now), 1, 1)
            keep = valid_ref[source][:1] * jnp.where(live, 1.0, 0.0)
            score = jnp.where(keep > 0.0, jnp.exp(logit * prior), 0.0)
            found.append((index, dest, mixed_now, message_now, logit, grad, score))
        for index, dest, mixed_now, message_now, logit, grad, score in found:
            mixed[index] = mixed_now
            message[index] = message_now
            logits[index] = logit
            prob_grad[index] = grad
            scores[index] = score
            sums[dest] += score
        return carry

    lax.fori_loop(0, edge_count // unroll, score_step, 0)
    for tile in range(dest_tiles):
        sums[tile] = 1.0 / head_sum(sums[tile])

    def delta_step(step, carry):
        found = []
        for part in range(unroll):
            index = step * unroll + part
            _, dest, _, _, _ = entry(index)
            soft = scores[index] * sums[dest]
            found.append((index, dest, soft, soft.astype(BF).astype(F32) * prob_grad[index]))
        for index, dest, soft, product in found:
            scores[index] = soft
            deltas[dest] += product
        return carry

    lax.fori_loop(0, edge_count // unroll, delta_step, 0)
    for tile in range(dest_tiles):
        deltas[tile] = head_sum(deltas[tile])

    def grad_step(step, carry):
        found = []
        for part in range(unroll):
            index = step * unroll + part
            _, dest, source, rel, prior = entry(index)
            at = rows_of(dest)
            soft = scores[index]
            score_grad = soft * (prob_grad[index] - deltas[dest])
            prior_now = jnp.sum(score_grad * logits[index], axis=0, keepdims=True)
            logit_grad = (score_grad * (prior * (TILE**-0.5))).astype(BF)
            query_now = mm(logit_grad, stacked(mixed[index]), 1, 0)
            mixed_grad = diagonal(mm(logit_grad, query_ref[at], 0, 0)).astype(BF)
            message_grad = diagonal(mm(soft.astype(BF), grad_ref[at], 0, 0)).astype(BF)
            key_now = mm(mixed_grad, wide[0, rel], 1, 1)
            value_now = mm(message_grad, wide[1, rel], 1, 1)
            score_weight = diagonal(mm(keys[rows_of(source)], mixed_grad, 0, 0))
            message_weight = diagonal(mm(values[rows_of(source)], message_grad, 0, 0))
            found.append(
                (
                    dest,
                    source,
                    rel,
                    prior_now,
                    query_now,
                    key_now,
                    value_now,
                    score_weight,
                    message_weight,
                )
            )
        for dest, source, rel, prior_now, query_now, key_now, value_now, one, two in found:
            prior_out[pl.ds(rel, 1)] += prior_now
            query_acc[dest] += query_now
            key_acc[source] += key_now
            value_acc[source] += value_now
            rel_out[rel] += one
            rel_out[RELS + rel] += two
        return carry

    lax.fori_loop(0, edge_count // unroll, grad_step, 0)
    for tile in range(dest_tiles):
        pack_out[tile * TILE : (tile + 1) * TILE] = query_acc[tile].astype(BF)
        at = own + tile * TILE
        pack_out[at : at + TILE] = key_acc[tile].astype(BF)
        at = 2 * own + tile * TILE
        pack_out[at : at + TILE] = value_acc[tile].astype(BF)
    empty = jnp.zeros((CAP, width), F32)
    slot_row = lax.broadcasted_iota(jnp.int32, (CAP, width), 0)
    for owner in range(halo_out.shape[0]):
        rows = empty
        for index in range(CAP):
            row = slot_ref[owner * CAP + index].astype(F32)
            rows = jnp.where(slot_row == index, row, rows)
        tile, at = dest_tiles + owner * CAP // TILE, owner * CAP % TILE
        halo_out[owner] = jnp.concatenate(
            [
                key_acc[tile, at : at + CAP],
                value_acc[tile, at : at + CAP],
                rows,
                empty,
            ],
            axis=0,
        ).astype(BF)


def attend(
    queries,
    key_rows,
    value_rows,
    halo_keys,
    halo_values,
    halo_rows,
    grad_output,
    edge_tiles,
    rel_weight,
    rel_prior,
    rel_blocks,
):
    own, width = queries.shape
    halo = halo_keys.shape[0]
    edges = edge_tiles.shape[0]
    dest_tiles = own // TILE
    source_tiles = (own + halo) // TILE
    unroll = 4 if edges % 4 == 0 else 1
    per_edge = (edges, TILE, width)
    per_dest = (dest_tiles, TILE, width)
    per_source = (source_tiles, TILE, width)
    return pl.pallas_call(
        functools.partial(attend_kernel, dest_tiles, source_tiles, edges, unroll),
        out_shape=(
            jax.ShapeDtypeStruct((3 * own, width), BF),
            jax.ShapeDtypeStruct((halo // CAP, 4 * CAP, width), BF),
            jax.ShapeDtypeStruct((rel_blocks, TILE, width), F32),
            jax.ShapeDtypeStruct((16, width), F32),
        ),
        in_specs=[SMEM] * 3 + [HBM] * 7,
        out_specs=(VMEM,) * 4,
        scratch_shapes=[
            pltpu.VMEM((own, width), BF),
            pltpu.VMEM((own, width), BF),
            pltpu.VMEM(rel_weight.shape, BF),
            pltpu.VMEM((own + halo, width), BF),
            pltpu.VMEM((own + halo, width), BF),
            pltpu.VMEM((2, RELS, width, width), BF),
            pltpu.VMEM(per_edge, BF),
            pltpu.VMEM(per_edge, BF),
            pltpu.VMEM(per_edge, F32),
            pltpu.VMEM(per_edge, F32),
            pltpu.VMEM(per_edge, F32),
            pltpu.VMEM(per_dest, F32),
            pltpu.VMEM(per_dest, F32),
            pltpu.VMEM(per_dest, F32),
            pltpu.VMEM(per_source, F32),
            pltpu.VMEM(per_source, F32),
            pltpu.VMEM((source_tiles, 8, width), F32),
            pltpu.SemaphoreType.DMA((7,)),
        ],
        compiler_params=pltpu.CompilerParams(vmem_limit_bytes=60 * 1024 * 1024),
        name="attend",
    )(
        edge_tiles.T,
        rel_prior.T,
        halo_rows,
        queries,
        key_rows,
        value_rows,
        halo_keys,
        halo_values,
        grad_output,
        rel_weight,
    )


def exchange_kernel(
    nodes,
    heads,
    shard,
    pack_ref,
    halo_ref,
    rel_ref,
    prior_ref,
    feats_ref,
    weight_hbm,
    types_ref,
    feats_out,
    proj_out,
    rel_final,
    prior_out,
    rel_out,
    pack,
    left_in,
    back_in,
    back,
    prior_in,
    rel_send,
    rel_in,
    rel_half,
    rel_half_bf,
    rel_parts,
    feat_acc,
    feat_send,
    feat_in,
    acc,
    part_send,
    part_in,
    weight_ref,
    local_sems,
    halo_sems,
    prior_sems,
    left_sems,
    share_sems,
    pack_sems,
    back_sems,
    pair_sems,
    split_sems,
    spread_sems,
    across_sems,
    head_sems,
    part_sems,
):
    lines = nodes // 2
    node = lax.axis_index("nodes")
    head = lax.axis_index("heads")
    line = node // 2
    side = node % 2
    own = feats_ref.shape[3]
    cuts = feats_ref.shape[1]
    width = pack.shape[2]
    slots = CAP * nodes
    half = rel_half.shape[0]
    piece = half // lines
    mesh = pl.DeviceIdType.MESH

    barrier = pltpu.get_barrier_semaphore()
    for step in range(1, nodes):
        peer = (lax.rem(node + step, nodes), head)
        pl.semaphore_signal(barrier, inc=1, device_id=peer, device_id_type=mesh)
    for step in range(1, heads):
        peer = (node, lax.rem(head + step, heads))
        pl.semaphore_signal(barrier, inc=1, device_id=peer, device_id_type=mesh)

    def copy(source, target, sems, index, to_node, to_head=None):
        return pltpu.make_async_remote_copy(
            src_ref=source,
            dst_ref=target,
            send_sem=sems.at[0, index],
            recv_sem=sems.at[1, index],
            device_id=(to_node, head if to_head is None else to_head),
            device_id_type=mesh,
        )

    def at_line(where):
        return where * 2 + side

    def travel(buffer, sems, step, act):
        block = line - step + 1

        @pl.when((line + 1 < lines) & (block >= 0))
        def _():
            here = buffer.at[block]
            act(
                pltpu.make_async_remote_copy(
                    src_ref=here,
                    dst_ref=here,
                    send_sem=sems.at[0, step],
                    recv_sem=sems.at[1, step],
                    device_id=(at_line(line + 1), head),
                    device_id_type=mesh,
                )
            )

        other = line + step - 1

        @pl.when((line >= 1) & (other < lines))
        def _():
            here = buffer.at[other]
            act(
                pltpu.make_async_remote_copy(
                    src_ref=here,
                    dst_ref=here,
                    send_sem=sems.at[2, step],
                    recv_sem=sems.at[3, step],
                    device_id=(at_line(line - 1), head),
                    device_id_type=mesh,
                )
            )

    def landed(buffer, sems, index, step, block):
        here = buffer.at[block]
        pltpu.make_async_remote_copy(
            src_ref=here,
            dst_ref=here,
            send_sem=sems.at[0, step],
            recv_sem=sems.at[index, step],
            device_id=(lax.rem(node + 1, nodes), head),
            device_id_type=mesh,
        ).wait_recv()

    def start(item):
        item.start()

    def wait_send(item):
        item.wait_send()

    loads = [
        pltpu.make_async_copy(weight_hbm, weight_ref, local_sems.at[0]),
        pltpu.make_async_copy(feats_ref.at[line], left_in.at[line], local_sems.at[1]),
    ]
    for load in loads:
        load.start()
    pack[line, : 3 * own] = pack_ref[...]
    blank = jnp.zeros((16 - own // width, width), F32)
    pack[line, 3 * own :] = jnp.concatenate([types_ref[...].astype(F32), blank], axis=0).astype(BF)
    back_in[node] = halo_ref[node]
    prior_in[node] = prior_ref[...]
    rel_send[...] = rel_ref[pl.ds(pl.multiple_of((1 - side) * half, 16), half)].astype(BF)
    pl.semaphore_wait(barrier, nodes + heads - 2)

    halo_copies, prior_copies, left_copies = [], [], []
    for step in range(1, nodes):
        to = lax.rem(node + step, nodes)
        halo_copies.append(copy(halo_ref.at[to], back_in.at[node], halo_sems, step, to))
        halo_copies[-1].start()
    pair = copy(rel_send, rel_in, pair_sems, 0, line * 2 + 1 - side)
    pair.start()
    travel(pack, pack_sems, 1, start)
    for step in range(1, lines):
        to = lax.rem(line + step, lines)
        here, there = feats_ref.at[to], left_in.at[line]
        if cuts > 1:
            here, there = here.at[head], there.at[head]
        left_copies.append(copy(here, there, left_sems, step, at_line(to)))
        left_copies[-1].start()
    for step in range(1, nodes):
        to = lax.rem(node + step, nodes)
        prior_copies.append(copy(prior_ref, prior_in.at[node], prior_sems, step, to))
        prior_copies[-1].start()

    def kinds_of(block):
        found = pack[block, 3 * own :].astype(F32)
        return jnp.concatenate([found[row : row + 1] for row in range(own // width)], axis=1)

    square = (own, own)
    even = lax.broadcasted_iota(jnp.int32, square, 0) == lax.broadcasted_iota(
        jnp.int32, square, 1
    )
    spread = jnp.where(even, kinds_of(line), 0.0).astype(BF)
    types = mm(spread, jnp.ones((own, width), BF), 1, 0)
    for load in loads:
        load.wait()
    type_masks = [(types == float(kind)).astype(F32).astype(BF) for kind in range(TYPES)]
    for group in range(3):
        rows = pack_ref[group * own : (group + 1) * own]
        total = sum(
            mm(rows * type_masks[kind], weight_ref[group, kind], 1, 1) for kind in range(TYPES)
        )
        if group == 0:
            feat_acc[...] = total
        else:
            feat_acc[...] += total

    for item in halo_copies:
        item.wait_recv()
    returned = back_in[...].astype(F32)
    key_back = returned[:, :CAP].reshape(slots, width).astype(BF)
    value_back = returned[:, CAP : 2 * CAP].reshape(slots, width).astype(BF)
    ids = returned[:, 2 * CAP : 3 * CAP].reshape(slots, width)
    back[line, :slots] = key_back
    back[line, slots : 2 * slots] = value_back
    back[line, 2 * slots :] = ids.astype(BF)
    travel(back, back_sems, 1, start)

    def chosen(found):
        wide = jnp.concatenate([found] * (own // width), axis=1)
        place = lax.broadcasted_iota(jnp.int32, (slots, own), 1).astype(F32)
        return (wide == place).astype(F32).astype(BF)

    pick = chosen(ids)
    feat_back = jnp.zeros((slots, feat_acc.shape[1]), F32)
    for kind in range(TYPES):
        kept = mm(pick, type_masks[kind], 1, 0).astype(BF)
        feat_back += mm(key_back * kept, weight_ref[1, kind], 1, 1)
        feat_back += mm(value_back * kept, weight_ref[2, kind], 1, 1)
    upper = feat_back.astype(BF)
    lower = (feat_back - upper.astype(F32)).astype(BF)
    feat_acc[...] += mm(pick, upper, 0, 0) + mm(pick, lower, 0, 0)
    for index in range(heads):
        feat_send[index] = feat_acc[:, index * width : (index + 1) * width].astype(BF)
    head_copies = []
    for step in range(1, heads):
        to = lax.rem(head + step, heads)
        head_copies.append(copy(feat_send.at[to], feat_in.at[step], head_sems, step, node, to))
        head_copies[-1].start()

    share_copies = []
    for step, item in enumerate(left_copies, 1):
        item.wait_recv()
        if cuts > 1:
            here = left_in.at[lax.rem(line - step + lines, lines), head]
            for other in range(1, heads):
                to = lax.rem(head + other, heads)
                index = step * heads + other
                share_copies.append(copy(here, here, share_sems, index, node, to))
                share_copies[-1].start()

    pair.wait_recv()
    own_half = rel_ref[pl.ds(pl.multiple_of(side * half, 16), half)]
    rel_half[...] = own_half + rel_in[...].astype(F32)
    rel_half_bf[...] = rel_half[...].astype(BF)
    split_copies = []
    for step in range(1, lines):
        to = lax.rem(line + step, lines)
        part = rel_half_bf.at[pl.ds(pl.multiple_of(to * piece, 16), piece)]
        split_copies.append(copy(part, rel_parts.at[step], split_sems, step, at_line(to)))
        split_copies[-1].start()

    acc[...] = jnp.zeros_like(acc)

    def gather_step(block):
        feats = left_in[block].reshape(2 * shard, own)
        kinds = kinds_of(block)
        masked = jnp.concatenate(
            [feats * (kinds == float(kind)).astype(F32).astype(BF) for kind in range(TYPES)],
            axis=0,
        )
        right = jnp.concatenate(
            [pack[block, group * own : (group + 1) * own] for group in range(3)], axis=1
        )
        acc[...] += mm(masked, right, 1, 0)
        return masked

    def return_step(block, masked):
        pick_now = chosen(back[block, 2 * slots :].astype(F32))
        taken = mm(masked, pick_now, 1, 1).astype(BF)
        right = jnp.concatenate([back[block, :slots], back[block, slots : 2 * slots]], axis=1)
        acc[:, width:] += mm(taken, right, 1, 0)

    return_step(line, gather_step(line))

    def across(slot):
        here = rel_out.at[side, slot]
        return copy(here, here, across_sems, slot, line * 2 + 1 - side)

    def send_across(slot):
        across(slot).start()

    def spread_step(step):
        behind, ahead = line - step, line + step

        @pl.when(behind >= 0)
        def _():
            landed(rel_out.at[side], spread_sems, 1, step, behind)

        @pl.when(ahead < lines)
        def _():
            landed(rel_out.at[side], spread_sems, 3, step, ahead)

        if step + 1 < lines:
            travel(rel_out.at[side], spread_sems, step + 1, start)

        @pl.when(behind >= 0)
        def _():
            send_across(behind)

        @pl.when(ahead < lines)
        def _():
            send_across(ahead)

    for item in share_copies:
        item.wait_recv()
    for step in range(1, lines):

        @pl.when(line - step >= 0)
        def _():
            landed(pack, pack_sems, 1, step, line - step)

        @pl.when(line + step < lines)
        def _():
            landed(pack, pack_sems, 3, step, line + step)

        if step + 1 < lines:
            travel(pack, pack_sems, step + 1, start)

        @pl.when(line - step >= 0)
        def _():
            landed(back, back_sems, 1, step, line - step)

        @pl.when(line + step < lines)
        def _():
            landed(back, back_sems, 3, step, line + step)

        if step + 1 < lines:
            travel(back, back_sems, step + 1, start)

        @pl.when(line - step >= 0)
        def _():
            return_step(line - step, gather_step(line - step))

        @pl.when(line + step < lines)
        def _():
            return_step(line + step, gather_step(line + step))

        if step == 1:
            for item in split_copies:
                item.wait_recv()
            final = rel_half[pl.ds(pl.multiple_of(line * piece, 16), piece)]
            for index in range(1, lines):
                final = final + rel_parts[index].astype(F32)
            rel_out[side, line] = final.astype(BF)
            travel(rel_out.at[side], spread_sems, 1, start)
            send_across(line)
        else:
            spread_step(step - 1)

    def share(of):
        return [
            acc[pl.ds(pl.multiple_of(kind * 2 * shard + of * shard, 8), shard)]
            for kind in range(TYPES)
        ]

    extra = part_send.shape[0] - TYPES * shard
    tail = [jnp.zeros((extra, acc.shape[1]), F32)] if extra else []
    part_send[...] = jnp.concatenate(share(1 - side) + tail, axis=0).astype(BF)
    part = copy(part_send, part_in, part_sems, 0, line * 2 + 1 - side)
    part.start()

    spread_step(lines - 1)

    for item in head_copies:
        item.wait_recv()
    mine = feat_acc[:, :width] * (head == 0).astype(F32)
    for index in range(1, heads):
        block = feat_acc[:, index * width : (index + 1) * width]
        mine = mine + block * (head == index).astype(F32)
    for step in range(1, heads):
        mine = mine + feat_in[step].astype(F32)
    feats_out[...] = mine.astype(BF)
    for item in prior_copies:
        item.wait_recv()
    total = prior_in[0]
    for index in range(1, nodes):
        total = total + prior_in[index]
    first = lax.broadcasted_iota(jnp.int32, total.shape, 1) < TILE
    one = jnp.sum(jnp.where(first, total, 0.0), axis=1, keepdims=True)
    two = jnp.sum(jnp.where(first, 0.0, total), axis=1, keepdims=True)
    flipped = jnp.where(first, one, two).T
    prior_out[...] = jnp.concatenate([flipped[:1], flipped[TILE : TILE + 1]], axis=0)

    part.wait_recv()
    other = part_in[...].astype(F32)
    for kind, rows in enumerate(share(side)):
        rows = rows + other[kind * shard : (kind + 1) * shard]
        for group in range(3):
            proj_out[group, kind] = rows[:, group * width : (group + 1) * width]
    for slot in range(lines):
        across(slot).wait()
    gathered = rel_out[...].astype(F32).reshape(2 * half, width)
    for kind in range(2):
        for rel in range(RELS):
            at = (kind * RELS + rel) * TILE
            for index in range(2):
                rel_final[kind, rel, index] = gathered[
                    at : at + TILE, index * TILE : (index + 1) * TILE
                ]

    sent = halo_copies + prior_copies + left_copies + head_copies + split_copies
    for item in sent + share_copies + [pair, part]:
        item.wait_send()
    for step in range(1, lines):
        travel(pack, pack_sems, step, wait_send)
        travel(back, back_sems, step, wait_send)
        travel(rel_out.at[side], spread_sems, step, wait_send)


def exchange(nodes, heads, pack, halo, rel, prior, feats, weight, types):
    own = feats.shape[3]
    width = pack.shape[1]
    lines = nodes // 2
    features = weight.shape[2]
    shard = features // nodes
    half = rel.shape[0] // 2
    piece = half // lines
    slots = CAP * nodes
    part_rows = -(-TYPES * shard // 16) * 16

    def sems(*dims):
        return pltpu.SemaphoreType.DMA(dims)

    return pl.pallas_call(
        functools.partial(exchange_kernel, nodes, heads, shard),
        out_shape=(
            jax.ShapeDtypeStruct((own, width), BF),
            jax.ShapeDtypeStruct((3, TYPES, shard, width), F32),
            jax.ShapeDtypeStruct((2, RELS, 2, TILE, TILE), F32),
            jax.ShapeDtypeStruct((2, 16), F32),
        ),
        in_specs=[VMEM] * 4 + [HBM] * 2 + [VMEM],
        out_specs=(VMEM,) * 4,
        scratch_shapes=[
            pltpu.VMEM((2, lines, piece, width), BF),
            pltpu.VMEM((lines, 3 * own + 16, width), BF),
            pltpu.VMEM((lines,) + feats.shape[1:], BF),
            pltpu.VMEM((nodes, 4 * CAP, width), BF),
            pltpu.VMEM((lines, 3 * slots, width), BF),
            pltpu.VMEM((nodes, 16, width), F32),
            pltpu.VMEM((half, width), BF),
            pltpu.VMEM((half, width), BF),
            pltpu.VMEM((half, width), F32),
            pltpu.VMEM((half, width), BF),
            pltpu.VMEM((lines, piece, width), BF),
            pltpu.VMEM((own, features), F32),
            pltpu.VMEM((heads, own, width), BF),
            pltpu.VMEM((heads, own, width), BF),
            pltpu.VMEM((TYPES * 2 * shard, 3 * width), F32),
            pltpu.VMEM((part_rows, 3 * width), BF),
            pltpu.VMEM((part_rows, 3 * width), BF),
            pltpu.VMEM(weight.shape, BF),
            sems(2),
            sems(2, nodes),
            sems(2, nodes),
            sems(2, lines),
            sems(2, lines * heads),
            sems(4, lines),
            sems(4, lines),
            sems(2, 1),
            sems(2, lines),
            sems(4, lines),
            sems(2, lines),
            sems(2, heads),
            sems(2, 1),
        ],
        compiler_params=pltpu.CompilerParams(
            collective_id=0, has_side_effects=True, vmem_limit_bytes=60 * 1024 * 1024
        ),
        name="exchange",
    )(pack, halo, rel, prior, feats, weight, types)


def per_device(
    nodes,
    heads,
    node_feats,
    node_types,
    queries,
    key_rows,
    value_rows,
    halo_keys,
    halo_values,
    halo_rows,
    edge_tiles,
    grad_output,
    proj_weight,
    rel_weight,
    rel_prior,
):
    own, features = node_feats.shape
    width = queries.shape[1]
    lines = nodes // 2
    shard = features // nodes
    piece = -(-2 * RELS * TILE // nodes // 16) * 16
    rel_rows = max(piece * nodes, 2 * RELS * TILE)
    pack, halo, rel, prior = attend(
        queries,
        key_rows,
        value_rows,
        halo_keys,
        halo_values,
        halo_rows,
        grad_output,
        edge_tiles,
        rel_weight,
        rel_prior,
        rel_rows // TILE,
    )
    cuts = heads if 2 * shard % (16 * heads) == 0 else 1
    feats = node_feats.T.reshape(lines, cuts, 2 * shard // cuts, own)
    types = node_types.reshape(own // width, width)
    grad_feats, proj, grad_rel, prior = exchange(
        nodes,
        heads,
        pack,
        halo,
        rel.reshape(rel_rows, width),
        prior,
        feats,
        proj_weight,
        types,
    )
    grad_proj = jnp.transpose(proj, (2, 0, 1, 3))
    grad_prior = prior[:, :RELS].T
    return (grad_feats, grad_proj, grad_rel, grad_prior)


def solution(mesh):
    return jax.shard_map(
        functools.partial(per_device, mesh.shape["nodes"], mesh.shape["heads"]),
        mesh=mesh,
        in_specs=(
            P("nodes", None),
            P("nodes"),
            P("nodes", "heads"),
            P("nodes", "heads"),
            P("nodes", "heads"),
            P("nodes", "heads"),
            P("nodes", "heads"),
            P("nodes"),
            P("nodes", None),
            P("nodes", "heads"),
            P(None, None, None, "heads"),
            P(None, None, "heads", None, None),
            P(None, "heads"),
        ),
        out_specs=(
            P("nodes", "heads"),
            P("nodes", None, None, "heads"),
            P(None, None, "heads", None, None),
            P(None, "heads"),
        ),
        check_vma=False,
    )
```

```python
import functools

import jax
import jax.numpy as jnp
from jax import lax
from jax.experimental import pallas as pl
from jax.experimental.pallas import tpu as pltpu
from jax.sharding import PartitionSpec as P

TYPES = 5
RELS = 15
TILE = 64
CAP = 8
BF = jnp.bfloat16
F32 = jnp.float32
VMEM = pl.BlockSpec(memory_space=pltpu.VMEM)
SMEM = pl.BlockSpec(memory_space=pltpu.SMEM)
HBM = pl.BlockSpec(memory_space=pltpu.HBM)


def mm(left, right, left_dim, right_dim):
    return lax.dot_general(
        left, right, (((left_dim,), (right_dim,)), ((), ())), preferred_element_type=F32
    )


def attend_kernel(
    dest_tiles,
    source_tiles,
    edge_count,
    unroll,
    edge_ref,
    prior_ref,
    slot_ref,
    query_hbm,
    key_hbm,
    value_hbm,
    halo_key_hbm,
    halo_value_hbm,
    grad_hbm,
    weight_hbm,
    pack_out,
    halo_out,
    rel_out,
    prior_out,
    query_ref,
    grad_ref,
    weight_ref,
    keys,
    values,
    wide,
    mixed,
    message,
    logits,
    scores,
    prob_grad,
    sums,
    deltas,
    query_acc,
    key_acc,
    value_acc,
    valid_ref,
    load_sems,
):
    own = dest_tiles * TILE
    halo = (source_tiles - dest_tiles) * TILE
    width = 2 * TILE
    loads = [
        pltpu.make_async_copy(source, target, load_sems.at[index])
        for index, (source, target) in enumerate(
            (
                (weight_hbm, weight_ref),
                (key_hbm, keys.at[:own]),
                (halo_key_hbm, keys.at[own:]),
                (value_hbm, values.at[:own]),
                (halo_value_hbm, values.at[own:]),
                (query_hbm, query_ref),
                (grad_hbm, grad_ref),
            )
        )
    ]
    for load in loads:
        load.start()
    for ref in (sums, deltas, query_acc, key_acc, value_acc, rel_out, prior_out):
        ref[...] = jnp.zeros_like(ref)
    lane = lax.broadcasted_iota(jnp.int32, (8, width), 1) % TILE
    for tile in range(dest_tiles):
        valid_ref[tile] = jnp.ones((8, width), F32)
    for tile in range(halo // TILE):
        found = jnp.zeros((8, width), F32)
        for index in range(TILE):
            inside = jnp.where(slot_ref[tile * TILE + index] < own, 1.0, 0.0)
            found = jnp.where(lane == index, inside, found)
        valid_ref[dest_tiles + tile] = found
    for load in loads:
        load.wait()
    blank = jnp.zeros((TILE, TILE), BF)
    for side in range(2):
        for rel in range(RELS):
            wide[side, rel] = jnp.concatenate(
                [
                    jnp.concatenate([weight_ref[side, rel, 0], blank], axis=1),
                    jnp.concatenate([blank, weight_ref[side, rel, 1]], axis=1),
                ],
                axis=0,
            )
    first = lax.broadcasted_iota(jnp.int32, (TILE, width), 1) < TILE
    first_row = lax.broadcasted_iota(jnp.int32, (1, width), 1) < TILE
    low = first.astype(F32).astype(BF)
    high = (1.0 - first.astype(F32)).astype(BF)

    def stacked(both):
        return jnp.concatenate([both * low, both * high], axis=0)

    def diagonal(square):
        return jnp.where(first, square[:TILE], square[TILE:])

    def head_sum(total):
        left = jnp.sum(jnp.where(first, total, 0.0), axis=1, keepdims=True)
        right = jnp.sum(jnp.where(first, 0.0, total), axis=1, keepdims=True)
        return jnp.where(first, left, right)

    def entry(index):
        target = edge_ref[0, index]
        live = target < dest_tiles
        dest = jnp.minimum(target, dest_tiles - 1)
        source = edge_ref[1, index]
        rel = edge_ref[2, index]
        prior = jnp.where(first_row, prior_ref[0, rel], prior_ref[1, rel])
        return live, dest, source, rel, prior

    def rows_of(tile):
        return pl.ds(pl.multiple_of(tile * TILE, TILE), TILE)

    def score_step(step, carry):
        found = []
        for part in range(unroll):
            index = step * unroll + part
            live, dest, source, rel, prior = entry(index)
            at = rows_of(dest)
            mixed_now = mm(keys[rows_of(source)], wide[0, rel], 1, 0).astype(BF)
            message_now = mm(values[rows_of(source)], wide[1, rel], 1, 0).astype(BF)
            logit = mm(query_ref[at], stacked(mixed_now), 1, 1) * (TILE**-0.5)
            grad = mm(grad_ref[at], stacked(message_now), 1, 1)
            keep = valid_ref[source][:1] * jnp.where(live, 1.0, 0.0)
            score = jnp.where(keep > 0.0, jnp.exp(logit * prior), 0.0)
            found.append((index, dest, mixed_now, message_now, logit, grad, score))
        for index, dest, mixed_now, message_now, logit, grad, score in found:
            mixed[index] = mixed_now
            message[index] = message_now
            logits[index] = logit
            prob_grad[index] = grad
            scores[index] = score
            sums[dest] += score
        return carry

    lax.fori_loop(0, edge_count // unroll, score_step, 0)
    for tile in range(dest_tiles):
        sums[tile] = 1.0 / head_sum(sums[tile])

    def delta_step(step, carry):
        found = []
        for part in range(unroll):
            index = step * unroll + part
            _, dest, _, _, _ = entry(index)
            soft = scores[index] * sums[dest]
            found.append((index, dest, soft, soft.astype(BF).astype(F32) * prob_grad[index]))
        for index, dest, soft, product in found:
            scores[index] = soft
            deltas[dest] += product
        return carry

    lax.fori_loop(0, edge_count // unroll, delta_step, 0)
    for tile in range(dest_tiles):
        deltas[tile] = head_sum(deltas[tile])

    def grad_step(step, carry):
        found = []
        for part in range(unroll):
            index = step * unroll + part
            _, dest, source, rel, prior = entry(index)
            at = rows_of(dest)
            soft = scores[index]
            score_grad = soft * (prob_grad[index] - deltas[dest])
            prior_now = jnp.sum(score_grad * logits[index], axis=0, keepdims=True)
            logit_grad = (score_grad * (prior * (TILE**-0.5))).astype(BF)
            query_now = mm(logit_grad, stacked(mixed[index]), 1, 0)
            mixed_grad = diagonal(mm(logit_grad, query_ref[at], 0, 0)).astype(BF)
            message_grad = diagonal(mm(soft.astype(BF), grad_ref[at], 0, 0)).astype(BF)
            key_now = mm(mixed_grad, wide[0, rel], 1, 1)
            value_now = mm(message_grad, wide[1, rel], 1, 1)
            score_weight = diagonal(mm(keys[rows_of(source)], mixed_grad, 0, 0))
            message_weight = diagonal(mm(values[rows_of(source)], message_grad, 0, 0))
            found.append(
                (
                    dest,
                    source,
                    rel,
                    prior_now,
                    query_now,
                    key_now,
                    value_now,
                    score_weight,
                    message_weight,
                )
            )
        for dest, source, rel, prior_now, query_now, key_now, value_now, one, two in found:
            prior_out[pl.ds(rel, 1)] += prior_now
            query_acc[dest] += query_now
            key_acc[source] += key_now
            value_acc[source] += value_now
            rel_out[rel] += one
            rel_out[RELS + rel] += two
        return carry

    lax.fori_loop(0, edge_count // unroll, grad_step, 0)
    for tile in range(dest_tiles):
        pack_out[tile * TILE : (tile + 1) * TILE] = query_acc[tile].astype(BF)
        at = own + tile * TILE
        pack_out[at : at + TILE] = key_acc[tile].astype(BF)
        at = 2 * own + tile * TILE
        pack_out[at : at + TILE] = value_acc[tile].astype(BF)
    empty = jnp.zeros((CAP, width), F32)
    slot_row = lax.broadcasted_iota(jnp.int32, (CAP, width), 0)
    for owner in range(halo_out.shape[0]):
        rows = empty
        for index in range(CAP):
            row = slot_ref[owner * CAP + index].astype(F32)
            rows = jnp.where(slot_row == index, row, rows)
        tile, at = dest_tiles + owner * CAP // TILE, owner * CAP % TILE
        halo_out[owner] = jnp.concatenate(
            [
                key_acc[tile, at : at + CAP],
                value_acc[tile, at : at + CAP],
                rows,
                empty,
            ],
            axis=0,
        ).astype(BF)


def attend(
    queries,
    key_rows,
    value_rows,
    halo_keys,
    halo_values,
    halo_rows,
    grad_output,
    edge_tiles,
    rel_weight,
    rel_prior,
    rel_blocks,
):
    own, width = queries.shape
    halo = halo_keys.shape[0]
    edges = edge_tiles.shape[0]
    dest_tiles = own // TILE
    source_tiles = (own + halo) // TILE
    unroll = 4 if edges % 4 == 0 else 1
    per_edge = (edges, TILE, width)
    per_dest = (dest_tiles, TILE, width)
    per_source = (source_tiles, TILE, width)
    return pl.pallas_call(
        functools.partial(attend_kernel, dest_tiles, source_tiles, edges, unroll),
        out_shape=(
            jax.ShapeDtypeStruct((3 * own, width), BF),
            jax.ShapeDtypeStruct((halo // CAP, 4 * CAP, width), BF),
            jax.ShapeDtypeStruct((rel_blocks, TILE, width), F32),
            jax.ShapeDtypeStruct((16, width), F32),
        ),
        in_specs=[SMEM] * 3 + [HBM] * 7,
        out_specs=(VMEM,) * 4,
        scratch_shapes=[
            pltpu.VMEM((own, width), BF),
            pltpu.VMEM((own, width), BF),
            pltpu.VMEM(rel_weight.shape, BF),
            pltpu.VMEM((own + halo, width), BF),
            pltpu.VMEM((own + halo, width), BF),
            pltpu.VMEM((2, RELS, width, width), BF),
            pltpu.VMEM(per_edge, BF),
            pltpu.VMEM(per_edge, BF),
            pltpu.VMEM(per_edge, F32),
            pltpu.VMEM(per_edge, F32),
            pltpu.VMEM(per_edge, F32),
            pltpu.VMEM(per_dest, F32),
            pltpu.VMEM(per_dest, F32),
            pltpu.VMEM(per_dest, F32),
            pltpu.VMEM(per_source, F32),
            pltpu.VMEM(per_source, F32),
            pltpu.VMEM((source_tiles, 8, width), F32),
            pltpu.SemaphoreType.DMA((7,)),
        ],
        compiler_params=pltpu.CompilerParams(vmem_limit_bytes=60 * 1024 * 1024),
        name="attend",
    )(
        edge_tiles.T,
        rel_prior.T,
        halo_rows,
        queries,
        key_rows,
        value_rows,
        halo_keys,
        halo_values,
        grad_output,
        rel_weight,
    )


def exchange_kernel(
    nodes,
    heads,
    shard,
    pack_ref,
    halo_ref,
    rel_ref,
    prior_ref,
    feats_ref,
    weight_hbm,
    types_ref,
    feats_out,
    proj_out,
    rel_final,
    prior_out,
    rel_out,
    pack,
    left_in,
    back_in,
    back,
    prior_in,
    rel_send,
    rel_in,
    rel_half,
    rel_half_bf,
    rel_parts,
    feat_acc,
    feat_send,
    feat_in,
    acc,
    part_send,
    part_in,
    weight_ref,
    local_sems,
    halo_sems,
    prior_sems,
    left_sems,
    share_sems,
    pack_sems,
    back_sems,
    pair_sems,
    split_sems,
    spread_sems,
    across_sems,
    head_sems,
    part_sems,
):
    lines = nodes // 2
    node = lax.axis_index("nodes")
    head = lax.axis_index("heads")
    line = node // 2
    side = node % 2
    own = feats_ref.shape[3]
    cuts = feats_ref.shape[1]
    width = pack.shape[2]
    slots = CAP * nodes
    half = rel_half.shape[0]
    piece = half // lines
    mesh = pl.DeviceIdType.MESH

    barrier = pltpu.get_barrier_semaphore()
    for step in range(1, nodes):
        peer = (lax.rem(node + step, nodes), head)
        pl.semaphore_signal(barrier, inc=1, device_id=peer, device_id_type=mesh)
    for step in range(1, heads):
        peer = (node, lax.rem(head + step, heads))
        pl.semaphore_signal(barrier, inc=1, device_id=peer, device_id_type=mesh)

    def copy(source, target, sems, index, to_node, to_head=None):
        return pltpu.make_async_remote_copy(
            src_ref=source,
            dst_ref=target,
            send_sem=sems.at[0, index],
            recv_sem=sems.at[1, index],
            device_id=(to_node, head if to_head is None else to_head),
            device_id_type=mesh,
        )

    def at_line(where):
        return where * 2 + side

    def travel(buffer, sems, step, act):
        block = line - step + 1

        @pl.when((line + 1 < lines) & (block >= 0))
        def _():
            here = buffer.at[block]
            act(
                pltpu.make_async_remote_copy(
                    src_ref=here,
                    dst_ref=here,
                    send_sem=sems.at[0, step],
                    recv_sem=sems.at[1, step],
                    device_id=(at_line(line + 1), head),
                    device_id_type=mesh,
                )
            )

        other = line + step - 1

        @pl.when((line >= 1) & (other < lines))
        def _():
            here = buffer.at[other]
            act(
                pltpu.make_async_remote_copy(
                    src_ref=here,
                    dst_ref=here,
                    send_sem=sems.at[2, step],
                    recv_sem=sems.at[3, step],
                    device_id=(at_line(line - 1), head),
                    device_id_type=mesh,
                )
            )

    def landed(buffer, sems, index, step, block):
        here = buffer.at[block]
        pltpu.make_async_remote_copy(
            src_ref=here,
            dst_ref=here,
            send_sem=sems.at[0, step],
            recv_sem=sems.at[index, step],
            device_id=(lax.rem(node + 1, nodes), head),
            device_id_type=mesh,
        ).wait_recv()

    def start(item):
        item.start()

    def wait_send(item):
        item.wait_send()

    loads = [
        pltpu.make_async_copy(weight_hbm, weight_ref, local_sems.at[0]),
        pltpu.make_async_copy(feats_ref.at[line], left_in.at[line], local_sems.at[1]),
    ]
    for load in loads:
        load.start()
    pack[line, : 3 * own] = pack_ref[...]
    blank = jnp.zeros((16 - own // width, width), F32)
    pack[line, 3 * own :] = jnp.concatenate([types_ref[...].astype(F32), blank], axis=0).astype(BF)
    back_in[node] = halo_ref[node]
    prior_in[node] = prior_ref[...]
    rel_send[...] = rel_ref[pl.ds(pl.multiple_of((1 - side) * half, 16), half)].astype(BF)
    pl.semaphore_wait(barrier, nodes + heads - 2)

    halo_copies, prior_copies, left_copies = [], [], []
    for step in range(1, nodes):
        to = lax.rem(node + step, nodes)
        halo_copies.append(copy(halo_ref.at[to], back_in.at[node], halo_sems, step, to))
        halo_copies[-1].start()
    pair = copy(rel_send, rel_in, pair_sems, 0, line * 2 + 1 - side)
    pair.start()
    travel(pack, pack_sems, 1, start)
    for step in range(1, lines):
        to = lax.rem(line + step, lines)
        here, there = feats_ref.at[to], left_in.at[line]
        if cuts > 1:
            here, there = here.at[head], there.at[head]
        left_copies.append(copy(here, there, left_sems, step, at_line(to)))
        left_copies[-1].start()
    for step in range(1, nodes):
        to = lax.rem(node + step, nodes)
        prior_copies.append(copy(prior_ref, prior_in.at[node], prior_sems, step, to))
        prior_copies[-1].start()

    def kinds_of(block):
        found = pack[block, 3 * own :].astype(F32)
        return jnp.concatenate([found[row : row + 1] for row in range(own // width)], axis=1)

    square = (own, own)
    even = lax.broadcasted_iota(jnp.int32, square, 0) == lax.broadcasted_iota(
        jnp.int32, square, 1
    )
    spread = jnp.where(even, kinds_of(line), 0.0).astype(BF)
    types = mm(spread, jnp.ones((own, width), BF), 1, 0)
    for load in loads:
        load.wait()
    type_masks = [(types == float(kind)).astype(F32).astype(BF) for kind in range(TYPES)]
    for group in range(3):
        rows = pack_ref[group * own : (group + 1) * own]
        total = sum(
            mm(rows * type_masks[kind], weight_ref[group, kind], 1, 1) for kind in range(TYPES)
        )
        if group == 0:
            feat_acc[...] = total
        else:
            feat_acc[...] += total

    for item in halo_copies:
        item.wait_recv()
    returned = back_in[...].astype(F32)
    key_back = returned[:, :CAP].reshape(slots, width).astype(BF)
    value_back = returned[:, CAP : 2 * CAP].reshape(slots, width).astype(BF)
    ids = returned[:, 2 * CAP : 3 * CAP].reshape(slots, width)
    back[line, :slots] = key_back
    back[line, slots : 2 * slots] = value_back
    back[line, 2 * slots :] = ids.astype(BF)
    travel(back, back_sems, 1, start)

    def chosen(found):
        wide = jnp.concatenate([found] * (own // width), axis=1)
        place = lax.broadcasted_iota(jnp.int32, (slots, own), 1).astype(F32)
        return (wide == place).astype(F32).astype(BF)

    pick = chosen(ids)
    feat_back = jnp.zeros((slots, feat_acc.shape[1]), F32)
    for kind in range(TYPES):
        kept = mm(pick, type_masks[kind], 1, 0).astype(BF)
        feat_back += mm(key_back * kept, weight_ref[1, kind], 1, 1)
        feat_back += mm(value_back * kept, weight_ref[2, kind], 1, 1)
    upper = feat_back.astype(BF)
    lower = (feat_back - upper.astype(F32)).astype(BF)
    feat_acc[...] += mm(pick, upper, 0, 0) + mm(pick, lower, 0, 0)
    for index in range(heads):
        feat_send[index] = feat_acc[:, index * width : (index + 1) * width].astype(BF)
    head_copies = []
    for step in range(1, heads):
        to = lax.rem(head + step, heads)
        head_copies.append(copy(feat_send.at[to], feat_in.at[step], head_sems, step, node, to))
        head_copies[-1].start()

    share_copies = []
    for step, item in enumerate(left_copies, 1):
        item.wait_recv()
        if cuts > 1:
            here = left_in.at[lax.rem(line - step + lines, lines), head]
            for other in range(1, heads):
                to = lax.rem(head + other, heads)
                index = step * heads + other
                share_copies.append(copy(here, here, share_sems, index, node, to))
                share_copies[-1].start()

    pair.wait_recv()
    own_half = rel_ref[pl.ds(pl.multiple_of(side * half, 16), half)]
    rel_half[...] = own_half + rel_in[...].astype(F32)
    rel_half_bf[...] = rel_half[...].astype(BF)
    split_copies = []
    for step in range(1, lines):
        to = lax.rem(line + step, lines)
        part = rel_half_bf.at[pl.ds(pl.multiple_of(to * piece, 16), piece)]
        split_copies.append(copy(part, rel_parts.at[step], split_sems, step, at_line(to)))
        split_copies[-1].start()

    acc[...] = jnp.zeros_like(acc)

    def gather_step(block):
        feats = left_in[block].reshape(2 * shard, own)
        kinds = kinds_of(block)
        masked = jnp.concatenate(
            [feats * (kinds == float(kind)).astype(F32).astype(BF) for kind in range(TYPES)],
            axis=0,
        )
        right = jnp.concatenate(
            [pack[block, group * own : (group + 1) * own] for group in range(3)], axis=1
        )
        acc[...] += mm(masked, right, 1, 0)
        return masked

    def return_step(block, masked):
        pick_now = chosen(back[block, 2 * slots :].astype(F32))
        taken = mm(masked, pick_now, 1, 1).astype(BF)
        right = jnp.concatenate([back[block, :slots], back[block, slots : 2 * slots]], axis=1)
        acc[:, width:] += mm(taken, right, 1, 0)

    return_step(line, gather_step(line))

    def across(slot):
        here = rel_out.at[side, slot]
        return copy(here, here, across_sems, slot, line * 2 + 1 - side)

    def send_across(slot):
        across(slot).start()

    def spread_step(step):
        behind, ahead = line - step, line + step

        @pl.when(behind >= 0)
        def _():
            landed(rel_out.at[side], spread_sems, 1, step, behind)

        @pl.when(ahead < lines)
        def _():
            landed(rel_out.at[side], spread_sems, 3, step, ahead)

        if step + 1 < lines:
            travel(rel_out.at[side], spread_sems, step + 1, start)

        @pl.when(behind >= 0)
        def _():
            send_across(behind)

        @pl.when(ahead < lines)
        def _():
            send_across(ahead)

    for item in share_copies:
        item.wait_recv()
    for step in range(1, lines):

        @pl.when(line - step >= 0)
        def _():
            landed(pack, pack_sems, 1, step, line - step)

        @pl.when(line + step < lines)
        def _():
            landed(pack, pack_sems, 3, step, line + step)

        if step + 1 < lines:
            travel(pack, pack_sems, step + 1, start)

        @pl.when(line - step >= 0)
        def _():
            landed(back, back_sems, 1, step, line - step)

        @pl.when(line + step < lines)
        def _():
            landed(back, back_sems, 3, step, line + step)

        if step + 1 < lines:
            travel(back, back_sems, step + 1, start)

        @pl.when(line - step >= 0)
        def _():
            return_step(line - step, gather_step(line - step))

        @pl.when(line + step < lines)
        def _():
            return_step(line + step, gather_step(line + step))

        if step == 1:
            for item in split_copies:
                item.wait_recv()
            final = rel_half[pl.ds(pl.multiple_of(line * piece, 16), piece)]
            for index in range(1, lines):
                final = final + rel_parts[index].astype(F32)
            rel_out[side, line] = final.astype(BF)
            travel(rel_out.at[side], spread_sems, 1, start)
            send_across(line)
        else:
            spread_step(step - 1)

    def share(of):
        return [
            acc[pl.ds(pl.multiple_of(kind * 2 * shard + of * shard, 8), shard)]
            for kind in range(TYPES)
        ]

    extra = part_send.shape[0] - TYPES * shard
    tail = [jnp.zeros((extra, acc.shape[1]), F32)] if extra else []
    part_send[...] = jnp.concatenate(share(1 - side) + tail, axis=0).astype(BF)
    part = copy(part_send, part_in, part_sems, 0, line * 2 + 1 - side)
    part.start()

    spread_step(lines - 1)

    for item in head_copies:
        item.wait_recv()
    mine = feat_acc[:, :width] * (head == 0).astype(F32)
    for index in range(1, heads):
        block = feat_acc[:, index * width : (index + 1) * width]
        mine = mine + block * (head == index).astype(F32)
    for step in range(1, heads):
        mine = mine + feat_in[step].astype(F32)
    feats_out[...] = mine.astype(BF)
    for item in prior_copies:
        item.wait_recv()
    total = prior_in[0]
    for index in range(1, nodes):
        total = total + prior_in[index]
    first = lax.broadcasted_iota(jnp.int32, total.shape, 1) < TILE
    one = jnp.sum(jnp.where(first, total, 0.0), axis=1, keepdims=True)
    two = jnp.sum(jnp.where(first, 0.0, total), axis=1, keepdims=True)
    flipped = jnp.where(first, one, two).T
    prior_out[...] = jnp.concatenate([flipped[:1], flipped[TILE : TILE + 1]], axis=0)

    part.wait_recv()
    other = part_in[...].astype(F32)
    for kind, rows in enumerate(share(side)):
        rows = rows + other[kind * shard : (kind + 1) * shard]
        for group in range(3):
            proj_out[group, kind] = rows[:, group * width : (group + 1) * width]
    for slot in range(lines):
        across(slot).wait()
    rel_final[...] = rel_out[...]

    sent = halo_copies + prior_copies + left_copies + head_copies + split_copies
    for item in sent + share_copies + [pair, part]:
        item.wait_send()
    for step in range(1, lines):
        travel(pack, pack_sems, step, wait_send)
        travel(back, back_sems, step, wait_send)
        travel(rel_out.at[side], spread_sems, step, wait_send)


def exchange(nodes, heads, pack, halo, rel, prior, feats, weight, types):
    own = feats.shape[3]
    width = pack.shape[1]
    lines = nodes // 2
    features = weight.shape[2]
    shard = features // nodes
    half = rel.shape[0] // 2
    piece = half // lines
    slots = CAP * nodes
    part_rows = -(-TYPES * shard // 16) * 16

    def sems(*dims):
        return pltpu.SemaphoreType.DMA(dims)

    return pl.pallas_call(
        functools.partial(exchange_kernel, nodes, heads, shard),
        out_shape=(
            jax.ShapeDtypeStruct((own, width), BF),
            jax.ShapeDtypeStruct((3, TYPES, shard, width), F32),
            jax.ShapeDtypeStruct((2, lines, piece, width), BF),
            jax.ShapeDtypeStruct((2, 16), F32),
        ),
        in_specs=[VMEM] * 4 + [HBM] * 2 + [VMEM],
        out_specs=(VMEM,) * 4,
        scratch_shapes=[
            pltpu.VMEM((2, lines, piece, width), BF),
            pltpu.VMEM((lines, 3 * own + 16, width), BF),
            pltpu.VMEM((lines,) + feats.shape[1:], BF),
            pltpu.VMEM((nodes, 4 * CAP, width), BF),
            pltpu.VMEM((lines, 3 * slots, width), BF),
            pltpu.VMEM((nodes, 16, width), F32),
            pltpu.VMEM((half, width), BF),
            pltpu.VMEM((half, width), BF),
            pltpu.VMEM((half, width), F32),
            pltpu.VMEM((half, width), BF),
            pltpu.VMEM((lines, piece, width), BF),
            pltpu.VMEM((own, features), F32),
            pltpu.VMEM((heads, own, width), BF),
            pltpu.VMEM((heads, own, width), BF),
            pltpu.VMEM((TYPES * 2 * shard, 3 * width), F32),
            pltpu.VMEM((part_rows, 3 * width), BF),
            pltpu.VMEM((part_rows, 3 * width), BF),
            pltpu.VMEM(weight.shape, BF),
            sems(2),
            sems(2, nodes),
            sems(2, nodes),
            sems(2, lines),
            sems(2, lines * heads),
            sems(4, lines),
            sems(4, lines),
            sems(2, 1),
            sems(2, lines),
            sems(4, lines),
            sems(2, lines),
            sems(2, heads),
            sems(2, 1),
        ],
        compiler_params=pltpu.CompilerParams(
            collective_id=0, has_side_effects=True, vmem_limit_bytes=60 * 1024 * 1024
        ),
        name="exchange",
    )(pack, halo, rel, prior, feats, weight, types)


def finish_kernel(feats_ref, proj_ref, rel_ref, prior_ref, feats_out, proj_out, rel_final, prior_out):
    feats_out[...] = feats_ref[...]
    proj_out[...] = proj_ref[...]
    prior_out[...] = prior_ref[:, :RELS]
    gathered = rel_ref[...].astype(F32).reshape(-1, rel_ref.shape[3])
    for kind in range(2):
        for rel in range(RELS):
            at = (kind * RELS + rel) * TILE
            for index in range(2):
                rel_final[kind, rel, index] = gathered[
                    at : at + TILE, index * TILE : (index + 1) * TILE
                ]


def finish(feats, proj, rel, prior):
    return pl.pallas_call(
        finish_kernel,
        out_shape=(
            jax.ShapeDtypeStruct(feats.shape, BF),
            jax.ShapeDtypeStruct(proj.shape, F32),
            jax.ShapeDtypeStruct((2, RELS, 2, TILE, TILE), F32),
            jax.ShapeDtypeStruct((2, RELS), F32),
        ),
        in_specs=[VMEM] * 4,
        out_specs=(VMEM,) * 4,
        compiler_params=pltpu.CompilerParams(vmem_limit_bytes=60 * 1024 * 1024),
        name="finish",
    )(feats, proj, rel, prior)


def per_device(
    nodes,
    heads,
    node_feats,
    node_types,
    queries,
    key_rows,
    value_rows,
    halo_keys,
    halo_values,
    halo_rows,
    edge_tiles,
    grad_output,
    proj_weight,
    rel_weight,
    rel_prior,
):
    own, features = node_feats.shape
    width = queries.shape[1]
    lines = nodes // 2
    shard = features // nodes
    piece = -(-2 * RELS * TILE // nodes // 16) * 16
    rel_rows = max(piece * nodes, 2 * RELS * TILE)
    pack, halo, rel, prior = attend(
        queries,
        key_rows,
        value_rows,
        halo_keys,
        halo_values,
        halo_rows,
        grad_output,
        edge_tiles,
        rel_weight,
        rel_prior,
        rel_rows // TILE,
    )
    cuts = heads if 2 * shard % (16 * heads) == 0 else 1
    feats = node_feats.T.reshape(lines, cuts, 2 * shard // cuts, own)
    types = node_types.reshape(own // width, width)
    grad_feats, proj, grad_rel, prior = exchange(
        nodes,
        heads,
        pack,
        halo,
        rel.reshape(rel_rows, width),
        prior,
        feats,
        proj_weight,
        types,
    )
    grad_feats, proj, grad_rel, prior = finish(grad_feats, proj, grad_rel, prior)
    grad_proj = jnp.transpose(proj, (2, 0, 1, 3))
    grad_prior = prior.T
    return (grad_feats, grad_proj, grad_rel, grad_prior)


def solution(mesh):
    return jax.shard_map(
        functools.partial(per_device, mesh.shape["nodes"], mesh.shape["heads"]),
        mesh=mesh,
        in_specs=(
            P("nodes", None),
            P("nodes"),
            P("nodes", "heads"),
            P("nodes", "heads"),
            P("nodes", "heads"),
            P("nodes", "heads"),
            P("nodes", "heads"),
            P("nodes"),
            P("nodes", None),
            P("nodes", "heads"),
            P(None, None, None, "heads"),
            P(None, None, "heads", None, None),
            P(None, "heads"),
        ),
        out_specs=(
            P("nodes", "heads"),
            P("nodes", None, None, "heads"),
            P(None, None, "heads", None, None),
            P(None, "heads"),
        ),
        check_vma=False,
    )
```
